1024 devices in a mesh: cap: 64 (over z, x_hi, core), rad: 16 (over y, x_lo).
Axes of the slice: x: 8 (x_hi: 4, x_lo: 2; x = x_hi * 2 + x_lo), y: 8, z: 8, core: 2. Of those that a mesh axis runs over, the one named last changes fastest.
Arguments:
- adjoint_velocity: float32 [3, 32, 64, 128, 128], P(None, 'rad', 'cap'), may hold values from -6 to 6
- adjoint_heat: float32 [32, 64, 128, 128], P('rad', 'cap'), may hold values from -6 to 6
- forcing: float32 [3, 32, 64, 128, 128], P(None, 'rad', 'cap'), may hold values from -6 to 6
- flow_velocity: float32 [3, 32, 64, 128, 128], P(None, 'rad', 'cap'), may hold values from -4 to 4
- forward_stress: float32 [3, 32, 64, 128, 128], P(None, 'rad', 'cap'), may hold values from -6 to 6
- viscosity: float32 [32, 64, 128, 128], P('rad', 'cap'), may hold values from 0.1 to 10
- layer_mask: int32 [32], P('rad'), may hold values 0 or 1
- face_flips: int32 [64, 4], replicated, may hold values from 0 to 1, as said below
Outputs:
- new_velocity: float32 [3, 32, 64, 128, 128], P(None, 'rad', 'cap')
- new_heat: float32 [32, 64, 128, 128], P('rad', 'cap')
- viscosity_gradient: float32 [64, 128, 128], P('cap', 'rad')
The draws below stay inside these ranges and needn't reach their ends.
Inputs may be any that keep to these rules, and one draw needn't show every extreme that they name: Equal on both sides of a shared edge: face_flips[t, 1] = face_flips[(t + 16) mod 64, 0] and face_flips[t, 3] = face_flips[(t + 1) mod 64, 2].
All inputs are finite; a program needn't handle non-finite values. No bound on the sum of `layer_mask` on one device may be relied on, other than what follows from the above.
Results may differ from the reference program's by a relative error of at most 0.00002.
Values sent between devices are 32-bit elements; how exact they have to be, the bound alone decides.
No kernel may reach another device: no remote copies, remote signals or barrier semaphores. Data moves between devices by JAX's collectives and lax.ppermute only.
A program may use at most 64 MiB of HBM per device.

```python
import math
import jax
import jax.numpy as jnp

S = 128
ITERS = 2
TILES = 64
NR = 32


def draw_face_flips(key, part):
    key = jax.random.fold_in(key, 2)
    flip_bits = jax.random.randint(key, (2, TILES), 0, 2).astype(jnp.int32)
    quarter = TILES // 4
    tile_ids = jnp.arange(TILES, dtype=jnp.int32)
    first = flip_bits[0][(tile_ids + TILES - quarter) % TILES]
    second = flip_bits[0][tile_ids]
    third = flip_bits[1][(tile_ids + TILES - 1) % TILES]
    fourth = flip_bits[1][tile_ids]
    return jnp.stack([first, second, third, fourth], axis=1).astype(jnp.int32)


def place_ends(array, own_key, least, largest):
    longest = array.shape.index(max(array.shape))
    spots = []
    for shift in (0, 1):
        where = [jax.random.randint(jax.random.fold_in(own_key, axis), (), 0, length) for axis, length in enumerate(array.shape)]
        where[longest] = (where[longest] + shift) % array.shape[longest]
        spots.append(tuple(where))
    return array.at[spots[0]].set(least).at[spots[1]].set(largest)


def steps_of(key, shape, split, least, high):
    level, own = 1.0, jax.random.fold_in(key, 6)
    for position, shards_of in split:
        draws = jnp.exp(jax.random.uniform(jax.random.fold_in(own, position), (shards_of,), jnp.float32, least / len(split), high / len(split)))
        level = level * jnp.repeat(draws, shape[position] // shards_of).reshape([-1 if axis == position else 1 for axis in range(len(shape))])
    return level


def bell_draw(rng, dims, deviation, bound, cuts=(), held_as=jnp.bfloat16):
    values = jax.random.normal(rng, dims, jnp.float32) * deviation
    if len(cuts) > 0:
        values = steps_of(rng, dims, cuts, -0.22, 0.18) * values
    return jnp.clip(values, min=-bound, max=bound).astype(held_as)


def setup_inputs(seed: int = 0) -> dict:
    keys = jax.random.split(jax.random.key(seed), 9)
    adjoint_velocity = bell_draw(keys[0], (3, NR, TILES, S, S), 1.0, 6.0, ((1, 16), (2, 64)), jnp.float32)
    adjoint_heat = bell_draw(keys[1], (NR, TILES, S, S), 1.0, 6.0, ((0, 16), (1, 64)), jnp.float32)
    forcing = bell_draw(keys[2], (3, NR, TILES, S, S), 1.0, 6.0, ((1, 16), (2, 64)), jnp.float32)
    flow_velocity = bell_draw(keys[3], (3, NR, TILES, S, S), 1.0, 4.0, ((1, 16), (2, 64)), jnp.float32)
    forward_stress = bell_draw(keys[4], (3, NR, TILES, S, S), 1.0, 6.0, ((1, 16), (2, 64)), jnp.float32)
    viscosity = jnp.clip(jnp.exp(math.log(10.0) - 4.6051702 * jax.random.uniform(keys[5], (NR, TILES, S, S), jnp.float32) ** steps_of(keys[5], (NR, TILES, S, S), ((0, 16), (1, 64)), -0.2, 0.2)), 0.1, 10.0)
    layer_mask = place_ends((jax.random.randint(keys[6], (NR,), 0, 3) < 1).astype(jnp.int32), jax.random.fold_in(keys[6], 1), 0, 1)
    face_flips = draw_face_flips(jax.random.fold_in(keys[8], 71), 0)
    return dict(adjoint_velocity=adjoint_velocity, adjoint_heat=adjoint_heat, forcing=forcing, flow_velocity=flow_velocity, forward_stress=forward_stress, viscosity=viscosity, layer_mask=layer_mask, face_flips=face_flips)


relaxation = 0.8
time_step = 0.1


def pick_face(edge_values, partners, flip_bits):
    chosen = jnp.take(edge_values, partners, axis=1)
    return jnp.where(flip_bits[:, None] == 1, chosen[..., ::-1], chosen)


def neighbours(field, face_flips):
    tile_ids = jnp.arange(TILES, dtype=jnp.int32)
    quarter = TILES // 4
    low_row = pick_face(field[:, :, -1, :], (tile_ids - quarter) % TILES, face_flips[:, 0])
    high_row = pick_face(field[:, :, 0, :], (tile_ids + quarter) % TILES, face_flips[:, 1])
    low_col = pick_face(field[:, :, :, -1], (tile_ids - 1) % TILES, face_flips[:, 2])
    high_col = pick_face(field[:, :, :, 0], (tile_ids + 1) % TILES, face_flips[:, 3])
    row_above = jnp.concatenate([low_row[:, :, None, :], field[:, :, :-1, :]], 2)
    row_below = jnp.concatenate([field[:, :, 1:, :], high_row[:, :, None, :]], 2)
    col_left = jnp.concatenate([low_col[..., None], field[..., :-1]], 3)
    col_right = jnp.concatenate([field[..., 1:], high_col[..., None]], 3)
    zero_layer = jnp.zeros_like(field[:1])
    layer_below = jnp.concatenate([zero_layer, field[:-1]], 0)
    layer_above = jnp.concatenate([field[1:], zero_layer], 0)
    return row_above, row_below, col_left, col_right, layer_below, layer_above


def advance(velocity, heat_field, totals, slopes, stiffness, forcing, flow_velocity):
    operator_image = stiffness * (6.0 * velocity - totals[:3]) + velocity
    drive = jnp.stack([forcing[0], forcing[1], forcing[2] + heat_field])
    moved = velocity + relaxation * (drive - operator_image) / (6.0 * stiffness + 1.0)
    carried = 0.5 * (flow_velocity[0] * slopes[0] + flow_velocity[1] * slopes[1] + flow_velocity[2] * slopes[2])
    warmed = heat_field + time_step * ((totals[3] - 6.0 * heat_field) + carried + velocity[2])
    return moved, warmed


def reference(adjoint_velocity, adjoint_heat, forcing, flow_velocity, forward_stress, viscosity, layer_mask, face_flips):
    stiffness = viscosity * (1.0 + 4.0 * layer_mask.astype(jnp.float32))[:, None, None, None]
    velocity = adjoint_velocity
    heat_field = adjoint_heat
    for iteration in range(ITERS):
        totals = []
        for component in range(3):
            parts = neighbours(velocity[component], face_flips)
            totals.append(parts[0] + parts[1] + parts[2] + parts[3] + parts[4] + parts[5])
        parts = neighbours(heat_field, face_flips)
        totals.append(parts[0] + parts[1] + parts[2] + parts[3] + parts[4] + parts[5])
        slopes = (parts[1] - parts[0], parts[3] - parts[2], parts[5] - parts[4])
        velocity, heat_field = advance(velocity, heat_field, jnp.stack(totals), slopes, stiffness, forcing, flow_velocity)
    gradient = jnp.sum(stiffness[None] * velocity * forward_stress, axis=(0, 1)) / (3.0 * NR)
    return velocity, heat_field, gradient
```

```python
import jax
import jax.numpy as jnp
from jax import lax
from jax.experimental import pallas as pl
from jax.experimental.pallas import tpu as pltpu
from jax.sharding import PartitionSpec as P

RELAX = 0.8
STEP = 0.1
VMEM_BYTES = 48 * 1024 * 1024


def lanes(shape):
    return lax.broadcasted_iota(jnp.int32, shape, len(shape) - 1)


def rows(shape):
    return lax.broadcasted_iota(jnp.int32, shape, len(shape) - 2)


def shifted(plane, by, axis):
    return pltpu.roll(plane, by % plane.shape[axis], axis)


def edge_columns(planes):
    count = len(planes)
    shape = planes[0].shape
    lane = lanes(shape)
    gathered = jnp.zeros(shape, jnp.float32)
    for k, plane in enumerate(planes):
        gathered = jnp.where(lane == k, shifted(plane, k, 1), gathered)
        gathered = jnp.where(lane == count + k, shifted(plane, count + k + 1, 1), gathered)
    return gathered.T[: 2 * count]


def pack_rims(planes, row_low, row_high, col_low, col_high):
    for k, plane in enumerate(planes):
        row_low[k : k + 1, :] = plane[0:1, :]
        row_high[k : k + 1, :] = plane[-1:, :]
    columns = edge_columns(planes)
    count = len(planes)
    col_low[...] = columns[:count]
    col_high[...] = columns[count:]


def pack_kernel(velocity, heat, lower, upper, row_low, row_high, col_low, col_high):
    planes = []
    for layer, out in enumerate((lower, upper)):
        for k in range(4):
            plane = velocity[k, layer] if k < 3 else heat[layer]
            out[k] = plane
            planes.append(plane)
    pack_rims(planes, row_low, row_high, col_low, col_high)


def turned(rim, flip):
    lane = lanes(rim.shape)
    return jnp.take_along_axis(rim, jnp.where(flip == 1, rim.shape[1] - 1 - lane, lane), axis=1)


def halos(flips, from_low_row, from_high_row, from_low_col, from_high_col):
    tile = lax.axis_index("cap")
    low_row = turned(from_low_row[...], flips[tile, 0])
    high_row = turned(from_high_row[...], flips[tile, 1])
    low_col = turned(from_low_col[...], flips[tile, 2]).T
    high_col = turned(from_high_col[...], flips[tile, 3]).T
    return low_row, high_row, low_col, high_col


def lateral(plane, k, rims):
    low_row, high_row, low_col, high_col = rims
    size = plane.shape[0]
    row, lane = rows(plane.shape), lanes(plane.shape)
    above = jnp.where(row == 0, low_row[k : k + 1, :], shifted(plane, 1, 0))
    below = jnp.where(row == size - 1, high_row[k : k + 1, :], shifted(plane, -1, 0))
    left = jnp.where(lane == 0, low_col[:, k : k + 1], shifted(plane, 1, 1))
    right = jnp.where(lane == size - 1, high_col[:, k : k + 1], shifted(plane, -1, 1))
    return above, below, left, right


def cycle_layer(layer, state, below_halo, above_halo, forcing, flow, stiffness, rims):
    own = state[layer]
    new = []
    weight = RELAX / (6.0 * stiffness + 1.0)
    heat = own[3]
    for k in range(4):
        plane = own[k]
        under = below_halo[k] if layer == 0 else state[0][k]
        over = above_halo[k] if layer == 1 else state[1][k]
        up, down, left, right = lateral(plane, layer * 4 + k, rims)
        total = up + down + left + right + under + over
        if k < 3:
            image = stiffness * (6.0 * plane - total) + plane
            drive = forcing[k, layer]
            if k == 2:
                drive = drive + heat
            new.append(plane + weight * (drive - image))
        else:
            carried = 0.5 * (
                flow[0, layer] * (down - up)
                + flow[1, layer] * (right - left)
                + flow[2, layer] * (over - under)
            )
            new.append(plane + STEP * (total - 6.0 * plane + carried + own[2]))
    return new


def stiffness_of(viscosity, mask, layer):
    return viscosity[layer] * (1.0 + 4.0 * mask[layer].astype(jnp.float32))


def first_kernel(
    flips, mask, lower, upper, below_halo, above_halo, lr, hr, lc, hc, forcing, flow, viscosity,
    new_lower, new_upper, row_low, row_high, col_low, col_high,
):
    rims = halos(flips, lr, hr, lc, hc)
    state = [[ref[k] for k in range(4)] for ref in (lower, upper)]
    planes = []
    for layer, out in enumerate((new_lower, new_upper)):
        new = cycle_layer(
            layer, state, below_halo, above_halo, forcing, flow,
            stiffness_of(viscosity, mask, layer), rims,
        )
        for k in range(4):
            out[k] = new[k]
        planes += new
    pack_rims(planes, row_low, row_high, col_low, col_high)


def last_kernel(
    flips, mask, lower, upper, below_halo, above_halo, lr, hr, lc, hc, forcing, flow, viscosity,
    stress, new_velocity, new_heat, partial,
):
    rims = halos(flips, lr, hr, lc, hc)
    state = [[ref[k] for k in range(4)] for ref in (lower, upper)]
    for layer in range(2):
        stiffness = stiffness_of(viscosity, mask, layer)
        new = cycle_layer(layer, state, below_halo, above_halo, forcing, flow, stiffness, rims)
        for k in range(3):
            new_velocity[k, layer] = new[k]
        new_heat[layer] = new[3]
        share = stiffness * (
            new[0] * stress[0, layer] + new[1] * stress[1, layer] + new[2] * stress[2, layer]
        )
        if layer == 0:
            partial[...] = share
        else:
            partial[...] = (partial[...] + share) * (1.0 / 96.0)


def call(kernel, outs, scalars, arrays):
    smem = pl.BlockSpec(memory_space=pltpu.SMEM)
    vmem = pl.BlockSpec(memory_space=pltpu.VMEM)
    return pl.pallas_call(
        kernel,
        out_shape=[jax.ShapeDtypeStruct(shape, jnp.float32) for shape in outs],
        in_specs=[smem] * len(scalars) + [vmem] * len(arrays),
        out_specs=[vmem] * len(outs),
        compiler_params=pltpu.CompilerParams(vmem_limit_bytes=VMEM_BYTES),
    )(*scalars, *arrays)


def around(array, by):
    count = lax.axis_size("cap")
    return lax.ppermute(array, "cap", [(i, (i + by) % count) for i in range(count)])


def along(array, by):
    count = lax.axis_size("rad")
    return lax.ppermute(
        array, "rad", [(i, i + by) for i in range(count) if 0 <= i + by < count]
    )


def exchange(lower, upper, row_low, row_high, col_low, col_high):
    quarter = lax.axis_size("cap") // 4
    below_halo = along(upper, 1)
    above_halo = along(lower, -1)
    from_low_row = around(row_high, quarter)
    from_high_row = around(row_low, -quarter)
    from_low_col = around(col_high, 1)
    from_high_col = around(col_low, -1)
    return below_halo, above_halo, from_low_row, from_high_row, from_low_col, from_high_col


def shards(
    adjoint_velocity, adjoint_heat, forcing, flow_velocity, forward_stress, viscosity, layer_mask,
    face_flips,
):
    size = adjoint_velocity.shape[-1]
    layer_shape = (4, size, size)
    rim_shape = (8, size)
    packed = [layer_shape] * 2 + [rim_shape] * 4
    velocity, heat = adjoint_velocity[:, :, 0], adjoint_heat[:, 0]
    forces, flow, stress, visc = (
        forcing[:, :, 0], flow_velocity[:, :, 0], forward_stress[:, :, 0], viscosity[:, 0]
    )
    scalars = (face_flips, layer_mask)
    state = call(pack_kernel, packed, (), (velocity, heat))
    received = exchange(*state)
    state = call(
        first_kernel, packed, scalars, (*state[:2], *received, forces, flow, visc)
    )
    received = exchange(*state)
    new_velocity, new_heat, partial = call(
        last_kernel,
        [velocity.shape, heat.shape, (size, size)],
        scalars,
        (*state[:2], *received, forces, flow, visc, stress),
    )
    count = lax.axis_size("rad")
    pieces = lax.all_to_all(partial, "rad", 0, 0, tiled=True)
    gradient = jnp.sum(pieces.reshape(count, size // count, size), axis=0)
    return new_velocity[:, :, None], new_heat[:, None], gradient[None]


def solution(mesh):
    fields = P(None, "rad", "cap", None, None)
    scalar_field = P("rad", "cap", None, None)
    return jax.shard_map(
        shards,
        mesh=mesh,
        in_specs=(
            fields, scalar_field, fields, fields, fields, scalar_field, P("rad"), P(),
        ),
        out_specs=(fields, scalar_field, P("cap", "rad", None)),
        check_vma=False,
    )
```

```python
import jax
import jax.numpy as jnp
from jax import lax
from jax.experimental import pallas as pl
from jax.experimental.pallas import tpu as pltpu
from jax.sharding import PartitionSpec as P

RELAX = 0.8
STEP = 0.1
VMEM_BYTES = 24 * 1024 * 1024


def lanes(shape):
    return lax.broadcasted_iota(jnp.int32, shape, len(shape) - 1)


def rows(shape):
    return lax.broadcasted_iota(jnp.int32, shape, len(shape) - 2)


def shifted(plane, by, axis):
    return pltpu.roll(plane, by % plane.shape[axis], axis)


def edge_columns(planes):
    count = len(planes)
    shape = planes[0].shape
    lane = lanes(shape)
    gathered = jnp.zeros(shape, jnp.float32)
    for k, plane in enumerate(planes):
        gathered = jnp.where(lane == k, shifted(plane, k, 1), gathered)
        gathered = jnp.where(lane == count + k, shifted(plane, count + k + 1, 1), gathered)
    return gathered.T[: 2 * count]


def pack_rims(planes, row_low, row_high, col_low, col_high):
    for k, plane in enumerate(planes):
        row_low[k : k + 1, :] = plane[0:1, :]
        row_high[k : k + 1, :] = plane[-1:, :]
    columns = edge_columns(planes)
    count = len(planes)
    col_low[...] = columns[:count]
    col_high[...] = columns[count:]


def pack_kernel(
    velocity, heat, mask, flips, lower, upper, row_low, row_high, col_low, col_high, facts,
    mask_here, flips_here, sems,
):
    copies = [
        pltpu.make_async_copy(mask, mask_here, sems.at[0]),
        pltpu.make_async_copy(flips, flips_here, sems.at[1]),
    ]
    for layer, out in enumerate((lower, upper)):
        copies.append(
            pltpu.make_async_copy(
                velocity.at[:, layer], out.at[pl.ds(0, 3)], sems.at[2 + 2 * layer]
            )
        )
        copies.append(
            pltpu.make_async_copy(heat.at[layer], out.at[3], sems.at[3 + 2 * layer])
        )
    for copy in copies:
        copy.start()
    for copy in copies:
        copy.wait()
    pack_rims(
        [ref[k] for ref in (lower, upper) for k in range(4)],
        row_low, row_high, col_low, col_high,
    )
    tile = lax.axis_index("cap")
    bits = flips_here[...]
    mine = jnp.sum(
        jnp.where(lanes(bits.shape) == tile, bits, 0).astype(jnp.float32), axis=1, keepdims=True
    )
    width = facts.shape[1]
    facts[0:4, :] = jnp.broadcast_to(mine, (4, width))
    for layer in range(2):
        scale = 1.0 + 4.0 * mask_here[layer].astype(jnp.float32)
        facts[4 + layer : 5 + layer, :] = jnp.full((1, width), scale, jnp.float32)


def turned(rim, flip):
    lane = lanes(rim.shape)
    picks = jnp.where(jnp.broadcast_to(flip, rim.shape) > 0.5, rim.shape[1] - 1 - lane, lane)
    return jnp.take_along_axis(rim, picks, axis=1)


def halos(facts, from_low_row, from_high_row, from_low_col, from_high_col):
    low_row = turned(from_low_row[...], facts[0:1, :])
    high_row = turned(from_high_row[...], facts[1:2, :])
    low_col = turned(from_low_col[...], facts[2:3, :]).T
    high_col = turned(from_high_col[...], facts[3:4, :]).T
    return low_row, high_row, low_col, high_col


def lateral(plane, k, rims):
    low_row, high_row, low_col, high_col = rims
    size = plane.shape[0]
    row, lane = rows(plane.shape), lanes(plane.shape)
    above = jnp.where(row == 0, low_row[k : k + 1, :], shifted(plane, 1, 0))
    below = jnp.where(row == size - 1, high_row[k : k + 1, :], shifted(plane, -1, 0))
    left = jnp.where(lane == 0, low_col[:, k : k + 1], shifted(plane, 1, 1))
    right = jnp.where(lane == size - 1, high_col[:, k : k + 1], shifted(plane, -1, 1))
    return above, below, left, right


def neighbours(layer, k, state, below_halo, above_halo, rims):
    under = below_halo[k] if layer == 0 else state[0][k]
    over = above_halo[k] if layer == 1 else state[1][k]
    return (*lateral(state[layer][k], layer * 4 + k, rims), under, over)


def moved(layer, state, below_halo, above_halo, forcing, stiffness, rims):
    new = []
    weight = RELAX / (6.0 * stiffness + 1.0)
    for k in range(3):
        plane = state[layer][k]
        total = sum(neighbours(layer, k, state, below_halo, above_halo, rims))
        image = stiffness * (6.0 * plane - total) + plane
        drive = forcing[k, layer]
        if k == 2:
            drive = drive + state[layer][3]
        new.append(plane + weight * (drive - image))
    return new


def warmed(layer, state, below_halo, above_halo, flow, rims):
    plane = state[layer][3]
    up, down, left, right, under, over = neighbours(
        layer, 3, state, below_halo, above_halo, rims
    )
    total = up + down + left + right + under + over
    carried = 0.5 * (
        flow[0, layer] * (down - up)
        + flow[1, layer] * (right - left)
        + flow[2, layer] * (over - under)
    )
    return plane + STEP * (total - 6.0 * plane + carried + state[layer][2])


def stiffness_of(viscosity, facts, layer):
    return viscosity[layer] * facts[4 + layer : 5 + layer, :]


def planes_of(lower, upper):
    return [[ref[k] for k in range(4)] for ref in (lower, upper)]


def first_kernel(
    facts, lower, upper, below_halo, above_halo, lr, hr, lc, hc, forcing, viscosity, flow_far,
    new_lower, new_upper, row_low, row_high, col_low, col_high, flow, sem,
):
    copy = pltpu.make_async_copy(flow_far, flow, sem)
    copy.start()
    rims = halos(facts, lr, hr, lc, hc)
    state = planes_of(lower, upper)
    planes = []
    for layer, out in enumerate((new_lower, new_upper)):
        new = moved(
            layer, state, below_halo, above_halo, forcing,
            stiffness_of(viscosity, facts, layer), rims,
        )
        for k in range(3):
            out[k] = new[k]
    copy.wait()
    for layer, out in enumerate((new_lower, new_upper)):
        out[3] = warmed(layer, state, below_halo, above_halo, flow, rims)
    planes = [ref[k] for ref in (new_lower, new_upper) for k in range(4)]
    pack_rims(planes, row_low, row_high, col_low, col_high)


def last_velocity_kernel(
    facts, lower, upper, below_halo, above_halo, lr, hr, lc, hc, forcing, viscosity, stress,
    new_velocity, partial,
):
    rims = halos(facts, lr, hr, lc, hc)
    state = planes_of(lower, upper)
    for layer in range(2):
        stiffness = stiffness_of(viscosity, facts, layer)
        new = moved(layer, state, below_halo, above_halo, forcing, stiffness, rims)
        for k in range(3):
            new_velocity[k, layer] = new[k]
        share = stiffness * (
            new[0] * stress[0, layer] + new[1] * stress[1, layer] + new[2] * stress[2, layer]
        )
        if layer == 0:
            partial[...] = share
        else:
            partial[...] = (partial[...] + share) * (1.0 / 96.0)


def last_heat_kernel(
    facts, lower, upper, below_halo, above_halo, lr, hr, lc, hc, velocity_near, flow_far,
    new_velocity, new_heat, flow, heat, sems,
):
    copies = [
        pltpu.make_async_copy(flow_far, flow, sems.at[0]),
        pltpu.make_async_copy(velocity_near, new_velocity, sems.at[1]),
    ]
    for copy in copies:
        copy.start()
    rims = halos(facts, lr, hr, lc, hc)
    state = planes_of(lower, upper)
    copies[0].wait()
    for layer in range(2):
        heat[layer] = warmed(layer, state, below_halo, above_halo, flow, rims)
    out = pltpu.make_async_copy(heat, new_heat, sems.at[2])
    out.start()
    copies[1].wait()
    out.wait()


VMEM = pl.BlockSpec(memory_space=pltpu.VMEM)
FAR = pl.BlockSpec(memory_space=pltpu.HBM)


def call(kernel, outs, near, far=(), scratch=(), out_specs=None, flops=0):
    far = [pltpu.with_memory_space_constraint(a, pltpu.HBM) for a in far]
    arrays = (*near, *far)
    moved_bytes = 4 * sum(a.size for a in arrays)
    return pl.pallas_call(
        kernel,
        out_shape=[jax.ShapeDtypeStruct(shape, jnp.float32) for shape in outs],
        in_specs=[VMEM] * len(near) + [FAR] * len(far),
        out_specs=out_specs or [VMEM] * len(outs),
        scratch_shapes=list(scratch),
        compiler_params=pltpu.CompilerParams(vmem_limit_bytes=VMEM_BYTES),
        cost_estimate=pl.CostEstimate(
            flops=flops, bytes_accessed=moved_bytes, transcendentals=0
        ),
    )(*arrays)


def around(array, by):
    count = lax.axis_size("cap")
    return lax.ppermute(array, "cap", [(i, (i + by) % count) for i in range(count)])


def along(array, by):
    count = lax.axis_size("rad")
    return lax.ppermute(
        array, "rad", [(i, i + by) for i in range(count) if 0 <= i + by < count]
    )


def exchange(lower, upper, row_low, row_high, col_low, col_high):
    quarter = lax.axis_size("cap") // 4
    below_halo = along(upper, 1)
    above_halo = along(lower, -1)
    from_low_row = around(row_high, quarter)
    from_high_row = around(row_low, -quarter)
    from_low_col = around(col_high, 1)
    from_high_col = around(col_low, -1)
    return below_halo, above_halo, from_low_row, from_high_row, from_low_col, from_high_col


def shards(
    adjoint_velocity, adjoint_heat, forcing, flow_velocity, forward_stress, viscosity, layer_mask,
    face_flips,
):
    size = adjoint_velocity.shape[-1]
    layer_shape = (4, size, size)
    rim_shape = (8, size)
    packed = [layer_shape] * 2 + [rim_shape] * 4
    velocity, heat = adjoint_velocity[:, :, 0], adjoint_heat[:, 0]
    forces, flow, stress, visc = (
        forcing[:, :, 0], flow_velocity[:, :, 0], forward_stress[:, :, 0], viscosity[:, 0]
    )
    flips = face_flips.T
    flow_here = pltpu.VMEM(flow.shape, jnp.float32)
    *state, facts = call(
        pack_kernel,
        packed + [rim_shape],
        (),
        (velocity, heat, layer_mask, flips),
        (
            pltpu.SMEM(layer_mask.shape, jnp.int32),
            pltpu.VMEM(flips.shape, jnp.int32),
            pltpu.SemaphoreType.DMA((6,)),
        ),
    )
    received = exchange(*state)
    state = call(
        first_kernel,
        packed,
        (facts, *state[:2], *received, forces, visc),
        (flow,),
        (flow_here, pltpu.SemaphoreType.DMA),
    )
    received = exchange(*state)
    near = (facts, *state[:2], *received)
    velocity_near, partial = call(
        last_velocity_kernel, [velocity.shape, (size, size)], (*near, forces, visc, stress)
    )
    pieces = lax.all_to_all(partial, "rad", 0, 0, tiled=True)
    new_velocity, new_heat = call(
        last_heat_kernel,
        [velocity.shape, heat.shape],
        (*near, velocity_near),
        (flow,),
        (flow_here, pltpu.VMEM(heat.shape, jnp.float32), pltpu.SemaphoreType.DMA((3,))),
        [FAR, FAR],
    )
    pieces, new_heat = lax.optimization_barrier((pieces, new_heat))
    count = lax.axis_size("rad")
    gradient = jnp.sum(pieces.reshape(count, size // count, size), axis=0)
    return new_velocity[:, :, None], new_heat[:, None], gradient[None]


def solution(mesh):
    fields = P(None, "rad", "cap", None, None)
    scalar_field = P("rad", "cap", None, None)
    return jax.shard_map(
        shards,
        mesh=mesh,
        in_specs=(
            fields, scalar_field, fields, fields, fields, scalar_field, P("rad"), P(),
        ),
        out_specs=(fields, scalar_field, P("cap", "rad", None)),
        check_vma=False,
    )
```

```python
import jax
import jax.numpy as jnp
from jax import lax
from jax.experimental import pallas as pl
from jax.experimental.pallas import tpu as pltpu
from jax.sharding import PartitionSpec as P

RELAX = 0.8
STEP = 0.1
VMEM_BYTES = 24 * 1024 * 1024


def lanes(shape):
    return lax.broadcasted_iota(jnp.int32, shape, len(shape) - 1)


def rows(shape):
    return lax.broadcasted_iota(jnp.int32, shape, len(shape) - 2)


def shifted(plane, by, axis):
    return pltpu.roll(plane, by % plane.shape[axis], axis)


def edge_columns(planes):
    count = len(planes)
    shape = planes[0].shape
    lane = lanes(shape)
    gathered = jnp.zeros(shape, jnp.float32)
    for k, plane in enumerate(planes):
        gathered = jnp.where(lane == k, shifted(plane, k, 1), gathered)
        gathered = jnp.where(lane == count + k, shifted(plane, count + k + 1, 1), gathered)
    return gathered.T[: 2 * count]


def plane_of(ref, k):
    size = ref.shape[1]
    return ref[k * size : (k + 1) * size, :]


EDGE, SECOND, STIFF, FORCE, FLOW, CORNERS = (slice(8 * n, 8 * n + 8) for n in range(6))
ROW_MESSAGE = 48
KEPT = 40


def pack_kernel(
    velocity, heat, mask, flips, forcing, flow, viscosity,
    lower, upper, row_low, row_high, col_low, col_high, facts,
    mask_here, flips_here, forcing_rims, flow_rims, viscosity_rims, sems, rim_sem,
):
    size = lower.shape[1]
    copies = [
        pltpu.make_async_copy(mask, mask_here, sems.at[0]),
        pltpu.make_async_copy(flips, flips_here, sems.at[1]),
    ]
    for layer, out in enumerate((lower, upper)):
        for k in range(4):
            copies.append(
                pltpu.make_async_copy(
                    velocity.at[k, layer] if k < 3 else heat.at[layer],
                    out.at[pl.ds(k * size, size)],
                    sems.at[2 + 4 * layer + k],
                )
            )
    for side, start in enumerate((0, size - 8)):
        for n, (source, target) in enumerate(
            ((forcing, forcing_rims), (flow, flow_rims), (viscosity, viscosity_rims))
        ):
            here = (slice(None),) * (len(source.shape) - 2) + (pl.ds(start, 8),)
            copies.append(
                pltpu.make_async_copy(
                    source.at[here], target.at[side], rim_sem.at[3 * side + n]
                )
            )
    for copy in copies:
        copy.start()
    for copy in copies:
        copy.wait()

    width = facts.shape[1]
    tiles = lax.axis_size("cap")
    tile = lax.axis_index("cap")
    bits = flips_here[...]
    row = rows(bits.shape)

    def bits_of(at):
        picked = jnp.where(lanes(bits.shape) == lax.rem(at + tiles, tiles), bits, 0)
        return jnp.sum(picked.astype(jnp.float32), axis=1, keepdims=True)

    facts[0:4, :] = jnp.broadcast_to(bits_of(tile), (4, width))
    facts[8:12, :] = jnp.broadcast_to(bits_of(tile - tiles // 4), (4, width))
    facts[12:16, :] = jnp.broadcast_to(bits_of(tile + tiles // 4), (4, width))
    for layer in range(2):
        scale = 1.0 + 4.0 * mask_here[layer].astype(jnp.float32)
        facts[4 + layer : 5 + layer, :] = jnp.full((1, width), scale, jnp.float32)

    planes = [plane_of(ref, k) for ref in (lower, upper) for k in range(4)]
    for side, (out, edge, second, rim) in enumerate(
        ((row_low, 0, 1, 0), (row_high, size - 1, size - 2, 7))
    ):
        for layer in range(2):
            scale = facts[4 + layer : 5 + layer, :]
            for k in range(4):
                at = 4 * layer + k
                plane = planes[at]
                out[at : at + 1, :] = plane[edge : edge + 1, :]
                out[8 + at : 9 + at, :] = plane[second : second + 1, :]
                if k < 3:
                    stiff = viscosity_rims[side, layer, rim : rim + 1, :] * scale
                    force = forcing_rims[side, k, layer, rim : rim + 1, :]
                    carry = jnp.zeros((1, width), jnp.float32)
                else:
                    stiff = flow_rims[side, 0, layer, rim : rim + 1, :]
                    force = flow_rims[side, 1, layer, rim : rim + 1, :]
                    carry = flow_rims[side, 2, layer, rim : rim + 1, :]
                out[16 + at : 17 + at, :] = stiff
                out[24 + at : 25 + at, :] = force
                out[32 + at : 33 + at, :] = carry
    first, last = row_low[EDGE, :], row_high[EDGE, :]
    lane = lanes(first.shape)
    corners = jnp.where(
        lane < 2,
        jnp.where(lane == 0, first, shifted(first, 2, 1)),
        jnp.where(lane == 2, shifted(last, 2, 1), shifted(last, 4, 1)),
    )
    row_low[CORNERS, :] = corners
    row_high[CORNERS, :] = corners
    columns = edge_columns(planes)
    col_low[...] = columns[:8]
    col_high[...] = columns[8:]


def turned(rim, flip):
    lane = lanes(rim.shape)
    picks = jnp.where(jnp.broadcast_to(flip, rim.shape) > 0.5, rim.shape[1] - 1 - lane, lane)
    return jnp.take_along_axis(rim, picks, axis=1)


def columns_of(facts, low, high):
    return turned(low[:8, :], facts[2:3, :]).T, turned(high[:8, :], facts[3:4, :]).T


def lateral(plane, k, rims):
    low_row, high_row, low_col, high_col = rims
    size = plane.shape[0]
    row, lane = rows(plane.shape), lanes(plane.shape)
    above = jnp.where(row == 0, low_row[k : k + 1, :], shifted(plane, 1, 0))
    below = jnp.where(row == size - 1, high_row[k : k + 1, :], shifted(plane, -1, 0))
    left = jnp.where(lane == 0, low_col[:, k : k + 1], shifted(plane, 1, 1))
    right = jnp.where(lane == size - 1, high_col[:, k : k + 1], shifted(plane, -1, 1))
    return above, below, left, right


def neighbours(layer, k, state, below_halo, above_halo, rims):
    under = plane_of(below_halo, k) if layer == 0 else state[0][k]
    over = plane_of(above_halo, k) if layer == 1 else state[1][k]
    return (*lateral(state[layer][k], layer * 4 + k, rims), under, over)


def moved(layer, state, below_halo, above_halo, forcing, stiffness, rims):
    new = []
    weight = RELAX / (6.0 * stiffness + 1.0)
    for k in range(3):
        plane = state[layer][k]
        total = sum(neighbours(layer, k, state, below_halo, above_halo, rims))
        image = stiffness * (6.0 * plane - total) + plane
        drive = forcing[k, layer]
        if k == 2:
            drive = drive + state[layer][3]
        new.append(plane + weight * (drive - image))
    return new


def warmed(layer, state, below_halo, above_halo, flow, rims):
    plane = state[layer][3]
    up, down, left, right, under, over = neighbours(
        layer, 3, state, below_halo, above_halo, rims
    )
    total = up + down + left + right + under + over
    carried = 0.5 * (
        flow[0, layer] * (down - up)
        + flow[1, layer] * (right - left)
        + flow[2, layer] * (over - under)
    )
    return plane + STEP * (total - 6.0 * plane + carried + state[layer][2])


def stiffness_of(viscosity, facts, layer):
    return viscosity[layer] * facts[4 + layer : 5 + layer, :]


def planes_of(lower, upper):
    return [[plane_of(ref, k) for k in range(4)] for ref in (lower, upper)]


def halo_row(message, own, below, above, left_end, right_end, flip, low):
    edge, second = message[EDGE], message[SECOND]
    lane, row = lanes(edge.shape), rows(edge.shape)
    left = jnp.where(lane == 0, left_end, shifted(edge, 1, 1))
    right = jnp.where(lane == edge.shape[1] - 1, right_end, shifted(edge, -1, 1))
    other = shifted(edge, 4, 0)
    under = jnp.where(row < 4, shifted(below, 4, 0), other)
    over = jnp.where(row < 4, other, shifted(above, 4, 0))
    total = own + second + left + right + under + over
    stiffness = message[STIFF]
    image = stiffness * (6.0 * edge - total) + edge
    field = row % 4
    drive = message[FORCE] + jnp.where(field == 2, shifted(edge, -1, 0), 0.0)
    velocity = edge + (RELAX / (6.0 * stiffness + 1.0)) * (drive - image)
    step_i = own - second if low else second - own
    step_j = (right - left) * (1.0 - 2.0 * flip)
    carried = 0.5 * (
        message[STIFF] * step_i + message[FORCE] * step_j + message[FLOW] * (over - under)
    )
    heat = edge + STEP * (total - 6.0 * edge + carried + shifted(edge, 1, 0))
    return jnp.where(field == 3, heat, velocity)


def halo_rows(facts, kept, row_low, row_high, below_halo, above_halo, low_col, high_col):
    size = facts.shape[1]
    below, above = below_halo[4 * size :, :], above_halo[4 * size :, :]
    at_low, at_high = low_col[8:16, :], high_col[8:16, :]

    def chosen(flag, corners, one, zero):
        flag = jnp.broadcast_to(facts[flag : flag + 1, 0:1], (8, 1))
        return jnp.where(flag > 0.5, corners[:, one : one + 1], corners[:, zero : zero + 1])

    made = []
    for side, own in enumerate((row_low, row_high)):
        flip = facts[side : side + 1, :]
        if side == 0:
            before = chosen(8 + 2, at_low, 1, 3)
            after = chosen(8 + 3, at_high, 0, 2)
        else:
            before = chosen(12 + 2, at_low, 4 + 3, 4 + 1)
            after = chosen(12 + 3, at_high, 4 + 2, 4 + 0)
        swap = jnp.broadcast_to(flip[:, 0:1], (8, 1)) > 0.5
        made.append(
            halo_row(
                kept[KEPT * side : KEPT * (side + 1), :],
                own[EDGE, :],
                below[8 * side : 8 * side + 8],
                above[8 * side : 8 * side + 8],
                jnp.where(swap, after, before),
                jnp.where(swap, before, after),
                flip,
                side == 0,
            )
        )
    return made


def first_kernel(
    facts, lower, upper, below_halo, above_halo, lr, hr, lc, hc, forcing, viscosity, flow_far,
    new_lower, new_upper, col_low, col_high, kept, flow, sem,
):
    copy = pltpu.make_async_copy(flow_far, flow, sem)
    copy.start()
    size = facts.shape[1]
    for side, message in enumerate((lr, hr)):
        kept[KEPT * side : KEPT * (side + 1), :] = turned(
            message[:KEPT, :], facts[side : side + 1, :]
        )
    edges = [kept[KEPT * side : KEPT * side + 8, :] for side in range(2)]
    rims = (*edges, *columns_of(facts, lc, hc))
    state = planes_of(lower, upper)
    outs = (new_lower, new_upper)
    for layer, out in enumerate(outs):
        new = moved(
            layer, state, below_halo, above_halo, forcing,
            stiffness_of(viscosity, facts, layer), rims,
        )
        for k in range(3):
            out[k * size : (k + 1) * size, :] = new[k]
        for side in range(2):
            out[4 * size + 8 * side : 4 * size + 8 * side + 8, :] = edges[side]
    copy.wait()
    for layer, out in enumerate(outs):
        out[3 * size : 4 * size, :] = warmed(layer, state, below_halo, above_halo, flow, rims)
    columns = edge_columns([plane_of(ref, k) for ref in outs for k in range(4)])
    corners = lr[CORNERS, :]
    corners = jnp.where(lanes(corners.shape) < 4, corners, shifted(hr[CORNERS, :], 4, 1))
    for n, out in enumerate((col_low, col_high)):
        out[0:8, :] = columns[8 * n : 8 * n + 8]
        out[8:16, :] = corners


def last_velocity_kernel(
    facts, lower, upper, below_halo, above_halo, lc, hc, kept, row_low, row_high, forcing,
    viscosity, stress, new_velocity, partial, edge_rows,
):
    edges = halo_rows(facts, kept, row_low, row_high, below_halo, above_halo, lc, hc)
    for side in range(2):
        edge_rows[8 * side : 8 * side + 8, :] = edges[side]
    rims = (*edges, *columns_of(facts, lc, hc))
    state = planes_of(lower, upper)
    for layer in range(2):
        stiffness = stiffness_of(viscosity, facts, layer)
        new = moved(layer, state, below_halo, above_halo, forcing, stiffness, rims)
        for k in range(3):
            new_velocity[k, layer] = new[k]
        share = stiffness * (
            new[0] * stress[0, layer] + new[1] * stress[1, layer] + new[2] * stress[2, layer]
        )
        if layer == 0:
            partial[...] = share
        else:
            partial[...] = (partial[...] + share) * (1.0 / 96.0)


def last_heat_kernel(
    facts, lower, upper, below_halo, above_halo, lc, hc, edge_rows, velocity_near, flow_far,
    new_velocity, new_heat, flow, heat, sems,
):
    copies = [
        pltpu.make_async_copy(flow_far, flow, sems.at[0]),
        pltpu.make_async_copy(velocity_near, new_velocity, sems.at[1]),
    ]
    for copy in copies:
        copy.start()
    rims = (edge_rows[0:8, :], edge_rows[8:16, :], *columns_of(facts, lc, hc))
    state = planes_of(lower, upper)
    copies[0].wait()
    for layer in range(2):
        heat[layer] = warmed(layer, state, below_halo, above_halo, flow, rims)
    out = pltpu.make_async_copy(heat, new_heat, sems.at[2])
    out.start()
    copies[1].wait()
    out.wait()


VMEM = pl.BlockSpec(memory_space=pltpu.VMEM)
FAR = pl.BlockSpec(memory_space=pltpu.HBM)


def call(kernel, outs, near, far=(), scratch=(), out_specs=None, flops=0):
    far = [pltpu.with_memory_space_constraint(a, pltpu.HBM) for a in far]
    arrays = (*near, *far)
    moved_bytes = 4 * sum(a.size for a in arrays)
    return pl.pallas_call(
        kernel,
        out_shape=[jax.ShapeDtypeStruct(shape, jnp.float32) for shape in outs],
        in_specs=[VMEM] * len(near) + [FAR] * len(far),
        out_specs=out_specs or [VMEM] * len(outs),
        scratch_shapes=list(scratch),
        compiler_params=pltpu.CompilerParams(vmem_limit_bytes=VMEM_BYTES),
        cost_estimate=pl.CostEstimate(
            flops=flops, bytes_accessed=moved_bytes, transcendentals=0
        ),
    )(*arrays)


def around(array, by):
    count = lax.axis_size("cap")
    return lax.ppermute(array, "cap", [(i, (i + by) % count) for i in range(count)])


def along(array, by):
    count = lax.axis_size("rad")
    return lax.ppermute(
        array, "rad", [(i, i + by) for i in range(count) if 0 <= i + by < count]
    )


def radial(lower, upper):
    return along(upper, 1), along(lower, -1)


def beside(low, high, step):
    return around(high, step), around(low, -step)


def shards(
    adjoint_velocity, adjoint_heat, forcing, flow_velocity, forward_stress, viscosity, layer_mask,
    face_flips,
):
    size = adjoint_velocity.shape[-1]
    quarter = lax.axis_size("cap") // 4
    velocity, heat = adjoint_velocity[:, :, 0], adjoint_heat[:, 0]
    forces, flow, stress, visc = (
        forcing[:, :, 0], flow_velocity[:, :, 0], forward_stress[:, :, 0], viscosity[:, 0]
    )
    flips = face_flips.T
    flow_here = pltpu.VMEM(flow.shape, jnp.float32)
    lower, upper, row_low, row_high, col_low, col_high, facts = call(
        pack_kernel,
        [(4 * size, size)] * 2 + [(ROW_MESSAGE, size)] * 2 + [(8, size)] * 2 + [(16, size)],
        (),
        (velocity, heat, layer_mask, flips, forces, flow, visc),
        (
            pltpu.SMEM(layer_mask.shape, jnp.int32),
            pltpu.VMEM(flips.shape, jnp.int32),
            pltpu.VMEM((2, 3, 2, 8, size), jnp.float32),
            pltpu.VMEM((2, 3, 2, 8, size), jnp.float32),
            pltpu.VMEM((2, 2, 8, size), jnp.float32),
            pltpu.SemaphoreType.DMA((10,)),
            pltpu.SemaphoreType.DMA((6,)),
        ),
    )
    halos = radial(lower, upper)
    rows_beside = beside(row_low, row_high, quarter)
    columns_beside = beside(col_low, col_high, 1)
    lower, upper, col_low, col_high, kept = call(
        first_kernel,
        [(4 * size + 16, size)] * 2 + [(16, size)] * 2 + [(2 * KEPT, size)],
        (facts, lower, upper, *halos, *rows_beside, *columns_beside, forces, visc),
        (flow,),
        (flow_here, pltpu.SemaphoreType.DMA),
    )
    near = (facts, lower, upper, *radial(lower, upper), *beside(col_low, col_high, 1))
    velocity_near, partial, edge_rows = call(
        last_velocity_kernel,
        [velocity.shape, (size, size), (16, size)],
        (*near, kept, row_low, row_high, forces, visc, stress),
    )
    pieces = lax.all_to_all(partial, "rad", 0, 0, tiled=True)
    new_velocity, new_heat = call(
        last_heat_kernel,
        [velocity.shape, heat.shape],
        (*near, edge_rows, velocity_near),
        (flow,),
        (flow_here, pltpu.VMEM(heat.shape, jnp.float32), pltpu.SemaphoreType.DMA((3,))),
        [FAR, FAR],
    )
    pieces, new_heat = lax.optimization_barrier((pieces, new_heat))
    count = lax.axis_size("rad")
    gradient = jnp.sum(pieces.reshape(count, size // count, size), axis=0)
    return new_velocity[:, :, None], new_heat[:, None], gradient[None]


def solution(mesh):
    fields = P(None, "rad", "cap", None, None)
    scalar_field = P("rad", "cap", None, None)
    return jax.shard_map(
        shards,
        mesh=mesh,
        in_specs=(
            fields, scalar_field, fields, fields, fields, scalar_field, P("rad"), P(),
        ),
        out_specs=(fields, scalar_field, P("cap", "rad", None)),
        check_vma=False,
    )
```

```python
import jax
import jax.numpy as jnp
from jax import lax
from jax.experimental import pallas as pl
from jax.experimental.pallas import tpu as pltpu
from jax.sharding import PartitionSpec as P

RELAX = 0.8
STEP = 0.1
VMEM_BYTES = 24 * 1024 * 1024


def lanes(shape):
    return lax.broadcasted_iota(jnp.int32, shape, len(shape) - 1)


def rows(shape):
    return lax.broadcasted_iota(jnp.int32, shape, len(shape) - 2)


def shifted(plane, by, axis):
    return pltpu.roll(plane, by % plane.shape[axis], axis)


def edge_columns(planes):
    count = len(planes)
    shape = planes[0].shape
    lane = lanes(shape)
    gathered = jnp.zeros(shape, jnp.float32)
    for k, plane in enumerate(planes):
        gathered = jnp.where(lane == k, shifted(plane, k, 1), gathered)
        gathered = jnp.where(lane == count + k, shifted(plane, count + k + 1, 1), gathered)
    return gathered.T[: 2 * count]


def plane_of(ref, k):
    size = ref.shape[1]
    return ref[k * size : (k + 1) * size, :]


EDGE, SECOND, STIFF, FORCE, FLOW, CORNERS = (slice(8 * n, 8 * n + 8) for n in range(6))
ROW_MESSAGE = 48
KEPT = 40


def core_index():
    return lax.rem(lax.axis_index("cap"), 2)


def in_order(from_partner, from_outside):
    second = core_index() == 1
    return (
        jnp.where(second, from_partner, from_outside),
        jnp.where(second, from_outside, from_partner),
    )


def pack_kernel(
    velocity, heat, mask, flips, forcing, flow, viscosity,
    lower, upper, row_own, gift, col_own, facts,
    mask_here, flips_here, forcing_rims, flow_rims, viscosity_rims, messages, cols, sems, rim_sem,
):
    size = lower.shape[1]
    row_low, row_high = messages.at[0], messages.at[1]
    core = core_index()
    copies = [
        pltpu.make_async_copy(mask, mask_here, sems.at[0]),
        pltpu.make_async_copy(flips, flips_here, sems.at[1]),
    ]
    for layer, out in enumerate((lower, upper)):
        for k in range(4):
            copies.append(
                pltpu.make_async_copy(
                    velocity.at[k, layer] if k < 3 else heat.at[layer],
                    out.at[pl.ds(k * size, size)],
                    sems.at[2 + 4 * layer + k],
                )
            )
    for side, start in enumerate((0, size - 8)):
        for n, (source, target) in enumerate(
            ((forcing, forcing_rims), (flow, flow_rims), (viscosity, viscosity_rims))
        ):
            here = (slice(None),) * (len(source.shape) - 2) + (pl.ds(start, 8),)
            copies.append(
                pltpu.make_async_copy(
                    source.at[here], target.at[side], rim_sem.at[3 * side + n]
                )
            )
    for copy in copies:
        copy.start()
    for copy in copies:
        copy.wait()

    width = facts.shape[1]
    tiles = lax.axis_size("cap")
    tile = lax.axis_index("cap")
    bits = flips_here[...]
    row = rows(bits.shape)

    def bits_of(at):
        picked = jnp.where(lanes(bits.shape) == lax.rem(at + tiles, tiles), bits, 0)
        return jnp.sum(picked.astype(jnp.float32), axis=1, keepdims=True)

    facts[0:4, :] = jnp.broadcast_to(bits_of(tile), (4, width))
    facts[8:12, :] = jnp.broadcast_to(bits_of(tile - tiles // 4), (4, width))
    facts[12:16, :] = jnp.broadcast_to(bits_of(tile + tiles // 4), (4, width))
    for layer in range(2):
        scale = 1.0 + 4.0 * mask_here[layer].astype(jnp.float32)
        facts[4 + layer : 5 + layer, :] = jnp.full((1, width), scale, jnp.float32)

    planes = [plane_of(ref, k) for ref in (lower, upper) for k in range(4)]
    for side, (out, edge, second, rim) in enumerate(
        ((row_low, 0, 1, 0), (row_high, size - 1, size - 2, 7))
    ):
        for layer in range(2):
            scale = facts[4 + layer : 5 + layer, :]
            for k in range(4):
                at = 4 * layer + k
                plane = planes[at]
                out[at : at + 1, :] = plane[edge : edge + 1, :]
                out[8 + at : 9 + at, :] = plane[second : second + 1, :]
                if k < 3:
                    stiff = viscosity_rims[side, layer, rim : rim + 1, :] * scale
                    force = forcing_rims[side, k, layer, rim : rim + 1, :]
                    carry = jnp.zeros((1, width), jnp.float32)
                else:
                    stiff = flow_rims[side, 0, layer, rim : rim + 1, :]
                    force = flow_rims[side, 1, layer, rim : rim + 1, :]
                    carry = flow_rims[side, 2, layer, rim : rim + 1, :]
                out[16 + at : 17 + at, :] = stiff
                out[24 + at : 25 + at, :] = force
                out[32 + at : 33 + at, :] = carry
    first, last = row_low[EDGE, :], row_high[EDGE, :]
    lane = lanes(first.shape)
    corners = jnp.where(
        lane < 2,
        jnp.where(lane == 0, first, shifted(first, 2, 1)),
        jnp.where(lane == 2, shifted(last, 2, 1), shifted(last, 4, 1)),
    )
    row_low[CORNERS, :] = corners
    row_high[CORNERS, :] = corners
    columns = edge_columns(planes)
    cols[0] = columns[:8]
    cols[1] = columns[8:]
    row_own[...] = messages[1 - core]
    gift[:ROW_MESSAGE, :] = messages[core]
    gift[ROW_MESSAGE:, :] = cols[1 - core]
    col_own[...] = cols[core]


def turned(rim, flip):
    lane = lanes(rim.shape)
    picks = jnp.where(jnp.broadcast_to(flip, rim.shape) > 0.5, rim.shape[1] - 1 - lane, lane)
    return jnp.take_along_axis(rim, picks, axis=1)


def columns_of(facts, low, high):
    return turned(low[:8], facts[2:3, :]).T, turned(high[:8], facts[3:4, :]).T


def lateral(plane, k, rims):
    low_row, high_row, low_col, high_col = rims
    size = plane.shape[0]
    row, lane = rows(plane.shape), lanes(plane.shape)
    above = jnp.where(row == 0, low_row[k : k + 1, :], shifted(plane, 1, 0))
    below = jnp.where(row == size - 1, high_row[k : k + 1, :], shifted(plane, -1, 0))
    left = jnp.where(lane == 0, low_col[:, k : k + 1], shifted(plane, 1, 1))
    right = jnp.where(lane == size - 1, high_col[:, k : k + 1], shifted(plane, -1, 1))
    return above, below, left, right


def neighbours(layer, k, state, below_halo, above_halo, rims):
    under = plane_of(below_halo, k) if layer == 0 else state[0][k]
    over = plane_of(above_halo, k) if layer == 1 else state[1][k]
    return (*lateral(state[layer][k], layer * 4 + k, rims), under, over)


def moved(layer, state, below_halo, above_halo, forcing, stiffness, rims):
    new = []
    weight = RELAX / (6.0 * stiffness + 1.0)
    for k in range(3):
        plane = state[layer][k]
        total = sum(neighbours(layer, k, state, below_halo, above_halo, rims))
        image = stiffness * (6.0 * plane - total) + plane
        drive = forcing[k, layer]
        if k == 2:
            drive = drive + state[layer][3]
        new.append(plane + weight * (drive - image))
    return new


def warmed(layer, state, below_halo, above_halo, flow, rims):
    plane = state[layer][3]
    up, down, left, right, under, over = neighbours(
        layer, 3, state, below_halo, above_halo, rims
    )
    total = up + down + left + right + under + over
    carried = 0.5 * (
        flow[0, layer] * (down - up)
        + flow[1, layer] * (right - left)
        + flow[2, layer] * (over - under)
    )
    return plane + STEP * (total - 6.0 * plane + carried + state[layer][2])


def stiffness_of(viscosity, facts, layer):
    return viscosity[layer] * facts[4 + layer : 5 + layer, :]


def planes_of(lower, upper):
    return [[plane_of(ref, k) for k in range(4)] for ref in (lower, upper)]


def halo_row(message, own, below, above, left_end, right_end, flip, low):
    edge, second = message[EDGE], message[SECOND]
    lane, row = lanes(edge.shape), rows(edge.shape)
    left = jnp.where(lane == 0, left_end, shifted(edge, 1, 1))
    right = jnp.where(lane == edge.shape[1] - 1, right_end, shifted(edge, -1, 1))
    other = shifted(edge, 4, 0)
    under = jnp.where(row < 4, shifted(below, 4, 0), other)
    over = jnp.where(row < 4, other, shifted(above, 4, 0))
    total = own + second + left + right + under + over
    stiffness = message[STIFF]
    image = stiffness * (6.0 * edge - total) + edge
    field = row % 4
    drive = message[FORCE] + jnp.where(field == 2, shifted(edge, -1, 0), 0.0)
    velocity = edge + (RELAX / (6.0 * stiffness + 1.0)) * (drive - image)
    step_i = own - second if low else second - own
    step_j = (right - left) * (1.0 - 2.0 * flip)
    carried = 0.5 * (
        message[STIFF] * step_i + message[FORCE] * step_j + message[FLOW] * (over - under)
    )
    heat = edge + STEP * (total - 6.0 * edge + carried + shifted(edge, 1, 0))
    return jnp.where(field == 3, heat, velocity)


def halo_rows(facts, kept, below_halo, above_halo, low_col, high_col):
    size = facts.shape[1]
    below, above = below_halo[4 * size :, :], above_halo[4 * size :, :]
    at_low, at_high = low_col[8:16], high_col[8:16]

    def chosen(flag, corners, one, zero):
        flag = jnp.broadcast_to(facts[flag : flag + 1, 0:1], (8, 1))
        return jnp.where(flag > 0.5, corners[:, one : one + 1], corners[:, zero : zero + 1])

    made = []
    for side in range(2):
        flip = facts[side : side + 1, :]
        if side == 0:
            before = chosen(8 + 2, at_low, 1, 3)
            after = chosen(8 + 3, at_high, 0, 2)
        else:
            before = chosen(12 + 2, at_low, 4 + 3, 4 + 1)
            after = chosen(12 + 3, at_high, 4 + 2, 4 + 0)
        swap = jnp.broadcast_to(flip[:, 0:1], (8, 1)) > 0.5
        made.append(
            halo_row(
                kept[KEPT * side : KEPT * (side + 1), :],
                kept[2 * KEPT + 8 * side : 2 * KEPT + 8 * side + 8, :],
                below[8 * side : 8 * side + 8],
                above[8 * side : 8 * side + 8],
                jnp.where(swap, after, before),
                jnp.where(swap, before, after),
                flip,
                side == 0,
            )
        )
    return made


def first_kernel(
    facts, lower, upper, below_halo, above_halo, gifts, got, passed, outer, forcing, viscosity,
    flow_far, new_lower, new_upper, col_given, col_own, kept, cols, flow, sem,
):
    copy = pltpu.make_async_copy(flow_far, flow, sem)
    copy.start()
    size = facts.shape[1]
    core = core_index()
    high, low = in_order(passed[1 - core], got[ROW_MESSAGE:, :])
    messages = (low, high)
    for side, message in enumerate(messages):
        kept[KEPT * side : KEPT * (side + 1), :] = turned(
            message[:KEPT], facts[side : side + 1, :]
        )
        edge = (size - 1) * side
        for layer, state in enumerate((lower, upper)):
            for k in range(4):
                at = 2 * KEPT + 8 * side + 4 * layer + k
                kept[at : at + 1, :] = state[k * size + edge : k * size + edge + 1, :]
    edges = [kept[KEPT * side : KEPT * side + 8, :] for side in range(2)]
    rims = (*edges, *columns_of(facts, *in_order(gifts[1 - core, ROW_MESSAGE:], outer[...])))
    state = planes_of(lower, upper)
    outs = (new_lower, new_upper)
    for layer, out in enumerate(outs):
        new = moved(
            layer, state, below_halo, above_halo, forcing,
            stiffness_of(viscosity, facts, layer), rims,
        )
        for k in range(3):
            out[k * size : (k + 1) * size, :] = new[k]
        for side in range(2):
            out[4 * size + 8 * side : 4 * size + 8 * side + 8, :] = edges[side]
    copy.wait()
    for layer, out in enumerate(outs):
        out[3 * size : 4 * size, :] = warmed(layer, state, below_halo, above_halo, flow, rims)
    columns = edge_columns([plane_of(ref, k) for ref in outs for k in range(4)])
    cols[0] = columns[:8]
    cols[1] = columns[8:]
    corners = [message[CORNERS] for message in messages]
    corners = jnp.where(lanes(corners[0].shape) < 4, corners[0], shifted(corners[1], 4, 1))
    col_given[:8, :] = cols[1 - core]
    col_own[:8, :] = cols[core]
    col_given[8:, :] = corners
    col_own[8:, :] = corners


def last_kernel(
    facts, lower, upper, below_halo, above_halo, gifts, outer, kept, forcing, viscosity, stress,
    flow, new_velocity, new_heat, partial, velocity, heat, sems,
):
    sides = in_order(gifts[1 - core_index()], outer[...])
    edges = halo_rows(facts, kept, below_halo, above_halo, *sides)
    rims = (*edges, *columns_of(facts, *sides))
    state = planes_of(lower, upper)
    copies = []

    def send(source, target):
        copies.append(pltpu.make_async_copy(source, target, sems.at[len(copies)]))
        copies[-1].start()

    for layer in range(2):
        heat[layer] = warmed(layer, state, below_halo, above_halo, flow, rims)
        send(heat.at[layer], new_heat.at[layer])
    for layer in range(2):
        stiffness = stiffness_of(viscosity, facts, layer)
        new = moved(layer, state, below_halo, above_halo, forcing, stiffness, rims)
        for k in range(3):
            velocity[k, layer] = new[k]
            send(velocity.at[k, layer], new_velocity.at[k, layer])
        share = stiffness * (
            new[0] * stress[0, layer] + new[1] * stress[1, layer] + new[2] * stress[2, layer]
        )
        if layer == 0:
            partial[...] = share
        else:
            partial[...] = (partial[...] + share) * (1.0 / 96.0)
    for copy in copies:
        copy.wait()


VMEM = pl.BlockSpec(memory_space=pltpu.VMEM)
FAR = pl.BlockSpec(memory_space=pltpu.HBM)


def call(kernel, outs, near, far=(), scratch=(), out_specs=None, flops=0):
    far = [pltpu.with_memory_space_constraint(a, pltpu.HBM) for a in far]
    arrays = (*near, *far)
    moved_bytes = 4 * sum(a.size for a in arrays)
    return pl.pallas_call(
        kernel,
        out_shape=[jax.ShapeDtypeStruct(shape, jnp.float32) for shape in outs],
        in_specs=[VMEM] * len(near) + [FAR] * len(far),
        out_specs=out_specs or [VMEM] * len(outs),
        scratch_shapes=list(scratch),
        compiler_params=pltpu.CompilerParams(vmem_limit_bytes=VMEM_BYTES),
        cost_estimate=pl.CostEstimate(
            flops=flops, bytes_accessed=moved_bytes, transcendentals=0
        ),
    )(*arrays)


def over_tiles(array, to):
    count = lax.axis_size("cap")
    return lax.ppermute(array, "cap", [(i, to(i) % count) for i in range(count)])


def of_chip(array):
    count = lax.axis_size("cap")
    pairs = [[i, i + 1] for i in range(0, count, 2)]
    return lax.all_gather(array, "cap", axis_index_groups=pairs)


def to_outer(array):
    return over_tiles(array, lambda i: i + 1 if i % 2 else i - 1)


def along(array, by):
    count = lax.axis_size("rad")
    return lax.ppermute(
        array, "rad", [(i, i + by) for i in range(count) if 0 <= i + by < count]
    )


def radial(lower, upper):
    return along(upper, 1), along(lower, -1)


def shards(
    adjoint_velocity, adjoint_heat, forcing, flow_velocity, forward_stress, viscosity, layer_mask,
    face_flips,
):
    size = adjoint_velocity.shape[-1]
    quarter = lax.axis_size("cap") // 4
    velocity, heat = adjoint_velocity[:, :, 0], adjoint_heat[:, 0]
    forces, flow, stress, visc = (
        forcing[:, :, 0], flow_velocity[:, :, 0], forward_stress[:, :, 0], viscosity[:, 0]
    )
    flips = face_flips.T
    f32 = jnp.float32
    lower, upper, row_own, gift, col_own, facts = call(
        pack_kernel,
        [(4 * size, size)] * 2
        + [(ROW_MESSAGE, size), (ROW_MESSAGE + 8, size), (8, size), (16, size)],
        (),
        (velocity, heat, layer_mask, flips, forces, flow, visc),
        (
            pltpu.SMEM(layer_mask.shape, jnp.int32),
            pltpu.VMEM(flips.shape, jnp.int32),
            pltpu.VMEM((2, 3, 2, 8, size), f32),
            pltpu.VMEM((2, 3, 2, 8, size), f32),
            pltpu.VMEM((2, 2, 8, size), f32),
            pltpu.VMEM((2, ROW_MESSAGE, size), f32),
            pltpu.VMEM((2, 8, size), f32),
            pltpu.SemaphoreType.DMA((10,)),
            pltpu.SemaphoreType.DMA((6,)),
        ),
    )
    halos = radial(lower, upper)
    gifts = of_chip(gift)
    core = lax.rem(lax.axis_index("cap"), 2)
    given = lax.dynamic_index_in_dim(gifts, 1 - core, 0, keepdims=False)[:ROW_MESSAGE]
    got = over_tiles(
        jnp.concatenate([row_own, given]),
        lambda i: i - quarter - 1 if i % 2 else i + quarter + 1,
    )
    outer = to_outer(col_own)
    passed = of_chip(got[:ROW_MESSAGE])
    lower, upper, col_given, col_own, kept = call(
        first_kernel,
        [(4 * size + 16, size)] * 2 + [(16, size)] * 2 + [(2 * KEPT + 16, size)],
        (facts, lower, upper, *halos, gifts, got, passed, outer, forces, visc),
        (flow,),
        (
            pltpu.VMEM((2, 8, size), f32),
            pltpu.VMEM(flow.shape, f32),
            pltpu.SemaphoreType.DMA,
        ),
    )
    halos = radial(lower, upper)
    gifts = of_chip(col_given)
    outer = to_outer(col_own)
    new_velocity, new_heat, partial = call(
        last_kernel,
        [velocity.shape, heat.shape, (size, size)],
        (facts, lower, upper, *halos, gifts, outer, kept, forces, visc, stress, flow),
        (),
        (
            pltpu.VMEM(velocity.shape, f32),
            pltpu.VMEM(heat.shape, f32),
            pltpu.SemaphoreType.DMA((8,)),
        ),
        [FAR, FAR, VMEM],
    )
    pieces = lax.all_to_all(partial, "rad", 0, 0, tiled=True)
    count = lax.axis_size("rad")
    gradient = jnp.sum(pieces.reshape(count, size // count, size), axis=0)
    return new_velocity[:, :, None], new_heat[:, None], gradient[None]


def solution(mesh):
    fields = P(None, "rad", "cap", None, None)
    scalar_field = P("rad", "cap", None, None)
    return jax.shard_map(
        shards,
        mesh=mesh,
        in_specs=(
            fields, scalar_field, fields, fields, fields, scalar_field, P("rad"), P(),
        ),
        out_specs=(fields, scalar_field, P("cap", "rad", None)),
        check_vma=False,
    )
```

```python
import jax
import jax.numpy as jnp
from jax import lax
from jax.experimental import pallas as pl
from jax.experimental.pallas import tpu as pltpu
from jax.sharding import PartitionSpec as P

RELAX = 0.8
STEP = 0.1
VMEM_BYTES = 24 * 1024 * 1024


def lanes(shape):
    return lax.broadcasted_iota(jnp.int32, shape, len(shape) - 1)


def rows(shape):
    return lax.broadcasted_iota(jnp.int32, shape, len(shape) - 2)


def shifted(plane, by, axis):
    return pltpu.roll(plane, by % plane.shape[axis], axis)


def evens(ref):
    return ref[pl.ds(0, 8, stride=2), :]


def odds(ref):
    return ref[pl.ds(1, 8, stride=2), :]


def edge_columns(planes, cols):
    shape = planes[0].shape
    half = lanes(shape) >> 1
    gathered = jnp.zeros(shape, jnp.float32)
    for k, plane in enumerate(planes):
        gathered = jnp.where(half == k, shifted(plane, 2 * k + 1, 1), gathered)
    cols[...] = gathered.T[:16]
    return odds(cols), evens(cols)


def plane_of(ref, k):
    size = ref.shape[1]
    return ref[k * size : (k + 1) * size, :]


EDGE, SECOND, STIFF, FORCE, FLOW, CORNERS = (slice(8 * n, 8 * n + 8) for n in range(6))
ROW_MESSAGE = 48
KEPT = 40


def core_index():
    return lax.rem(lax.axis_index("cap"), 2)


def in_order(from_partner, from_outside):
    second = core_index() == 1
    return (
        jnp.where(second, from_partner, from_outside),
        jnp.where(second, from_outside, from_partner),
    )


def pack_kernel(
    velocity, heat, mask, flips, forcing, flow, viscosity,
    lower, upper, row_own, gift, col_own, facts,
    mask_here, flips_here, forcing_rims, flow_rims, viscosity_rims, messages, cols, sems, rim_sem,
):
    size = lower.shape[1]
    row_low, row_high = messages.at[0], messages.at[1]
    core = core_index()
    copies = [
        pltpu.make_async_copy(mask, mask_here, sems.at[0]),
        pltpu.make_async_copy(flips, flips_here, sems.at[1]),
    ]
    for layer, out in enumerate((lower, upper)):
        for k in range(4):
            copies.append(
                pltpu.make_async_copy(
                    velocity.at[k, layer] if k < 3 else heat.at[layer],
                    out.at[pl.ds(k * size, size)],
                    sems.at[2 + 4 * layer + k],
                )
            )
    for side, start in enumerate((0, size - 8)):
        for n, (source, target) in enumerate(
            ((forcing, forcing_rims), (flow, flow_rims), (viscosity, viscosity_rims))
        ):
            here = (slice(None),) * (len(source.shape) - 2) + (pl.ds(start, 8),)
            copies.append(
                pltpu.make_async_copy(
                    source.at[here], target.at[side], rim_sem.at[3 * side + n]
                )
            )
    for copy in copies:
        copy.start()
    for copy in copies:
        copy.wait()

    width = facts.shape[1]
    tiles = lax.axis_size("cap")
    tile = lax.axis_index("cap")
    bits = flips_here[...]
    row = rows(bits.shape)

    def bits_of(at):
        picked = jnp.where(lanes(bits.shape) == lax.rem(at + tiles, tiles), bits, 0)
        return jnp.sum(picked.astype(jnp.float32), axis=1, keepdims=True)

    facts[0:4, :] = jnp.broadcast_to(bits_of(tile), (4, width))
    facts[8:12, :] = jnp.broadcast_to(bits_of(tile - tiles // 4), (4, width))
    facts[12:16, :] = jnp.broadcast_to(bits_of(tile + tiles // 4), (4, width))
    for layer in range(2):
        scale = 1.0 + 4.0 * mask_here[layer].astype(jnp.float32)
        facts[4 + layer : 5 + layer, :] = jnp.full((1, width), scale, jnp.float32)

    planes = [plane_of(ref, k) for ref in (lower, upper) for k in range(4)]
    for side, (out, edge, second, rim) in enumerate(
        ((row_low, 0, 1, 0), (row_high, size - 1, size - 2, 7))
    ):
        for layer in range(2):
            scale = facts[4 + layer : 5 + layer, :]
            for k in range(4):
                at = 4 * layer + k
                plane = planes[at]
                out[at : at + 1, :] = plane[edge : edge + 1, :]
                out[8 + at : 9 + at, :] = plane[second : second + 1, :]
                if k < 3:
                    stiff = viscosity_rims[side, layer, rim : rim + 1, :] * scale
                    force = forcing_rims[side, k, layer, rim : rim + 1, :]
                    carry = jnp.zeros((1, width), jnp.float32)
                else:
                    stiff = flow_rims[side, 0, layer, rim : rim + 1, :]
                    force = flow_rims[side, 1, layer, rim : rim + 1, :]
                    carry = flow_rims[side, 2, layer, rim : rim + 1, :]
                out[16 + at : 17 + at, :] = stiff
                out[24 + at : 25 + at, :] = force
                out[32 + at : 33 + at, :] = carry
    first, last = row_low[EDGE, :], row_high[EDGE, :]
    lane = lanes(first.shape)
    corners = jnp.where(
        lane < 2,
        jnp.where(lane == 0, first, shifted(first, 2, 1)),
        jnp.where(lane == 2, shifted(last, 2, 1), shifted(last, 4, 1)),
    )
    row_low[CORNERS, :] = corners
    row_high[CORNERS, :] = corners
    low, high = edge_columns(planes, cols)
    row_own[...] = messages[1 - core]
    gift[:ROW_MESSAGE, :] = messages[core]
    gift[ROW_MESSAGE:, :], col_own[...] = in_order(high, low)[::-1]


def turned(rim, flip):
    lane = lanes(rim.shape)
    picks = jnp.where(jnp.broadcast_to(flip, rim.shape) > 0.5, rim.shape[1] - 1 - lane, lane)
    return jnp.take_along_axis(rim, picks, axis=1)


def columns_of(facts, low, high, cols):
    cols[pl.ds(0, 8, stride=2), :] = turned(high[:8], facts[3:4, :])
    cols[pl.ds(1, 8, stride=2), :] = turned(low[:8], facts[2:3, :])
    size = facts.shape[1]
    rest = jnp.zeros((size - 16, size), jnp.float32)
    return jnp.concatenate([cols[...], rest], 0).T


def lateral(plane, k, rims):
    low_row, high_row, columns = rims
    size = plane.shape[0]
    ends = shifted(columns, -(2 * k + 1), 1)
    row, lane = rows(plane.shape), lanes(plane.shape)
    above = jnp.where(row == 0, low_row[k : k + 1, :], shifted(plane, 1, 0))
    below = jnp.where(row == size - 1, high_row[k : k + 1, :], shifted(plane, -1, 0))
    left = jnp.where(lane == 0, ends, shifted(plane, 1, 1))
    right = jnp.where(lane == size - 1, ends, shifted(plane, -1, 1))
    return above, below, left, right


def neighbours(layer, k, state, below_halo, above_halo, rims):
    under = plane_of(below_halo, k) if layer == 0 else state[0][k]
    over = plane_of(above_halo, k) if layer == 1 else state[1][k]
    return (*lateral(state[layer][k], layer * 4 + k, rims), under, over)


def moved(layer, state, below_halo, above_halo, forcing, stiffness, rims):
    new = []
    weight = RELAX / (6.0 * stiffness + 1.0)
    for k in range(3):
        plane = state[layer][k]
        total = sum(neighbours(layer, k, state, below_halo, above_halo, rims))
        image = stiffness * (6.0 * plane - total) + plane
        drive = forcing[k, layer]
        if k == 2:
            drive = drive + state[layer][3]
        new.append(plane + weight * (drive - image))
    return new


def warmed(layer, state, below_halo, above_halo, flow, rims):
    plane = state[layer][3]
    up, down, left, right, under, over = neighbours(
        layer, 3, state, below_halo, above_halo, rims
    )
    total = up + down + left + right + under + over
    carried = 0.5 * (
        flow[0, layer] * (down - up)
        + flow[1, layer] * (right - left)
        + flow[2, layer] * (over - under)
    )
    return plane + STEP * (total - 6.0 * plane + carried + state[layer][2])


def stiffness_of(viscosity, facts, layer):
    return viscosity[layer] * facts[4 + layer : 5 + layer, :]


def planes_of(lower, upper):
    return [[plane_of(ref, k) for k in range(4)] for ref in (lower, upper)]


def halo_row(message, own, below, above, left_end, right_end, flip, low):
    edge, second = message[EDGE], message[SECOND]
    lane, row = lanes(edge.shape), rows(edge.shape)
    left = jnp.where(lane == 0, left_end, shifted(edge, 1, 1))
    right = jnp.where(lane == edge.shape[1] - 1, right_end, shifted(edge, -1, 1))
    other = shifted(edge, 4, 0)
    under = jnp.where(row < 4, shifted(below, 4, 0), other)
    over = jnp.where(row < 4, other, shifted(above, 4, 0))
    total = own + second + left + right + under + over
    stiffness = message[STIFF]
    image = stiffness * (6.0 * edge - total) + edge
    field = row % 4
    drive = message[FORCE] + jnp.where(field == 2, shifted(edge, -1, 0), 0.0)
    velocity = edge + (RELAX / (6.0 * stiffness + 1.0)) * (drive - image)
    step_i = own - second if low else second - own
    step_j = (right - left) * (1.0 - 2.0 * flip)
    carried = 0.5 * (
        message[STIFF] * step_i + message[FORCE] * step_j + message[FLOW] * (over - under)
    )
    heat = edge + STEP * (total - 6.0 * edge + carried + shifted(edge, 1, 0))
    return jnp.where(field == 3, heat, velocity)


def halo_rows(facts, kept, below_halo, above_halo, low_col, high_col):
    size = facts.shape[1]
    below, above = below_halo[4 * size :, :], above_halo[4 * size :, :]
    at_low, at_high = low_col[8:16], high_col[8:16]

    def chosen(flag, corners, one, zero):
        flag = jnp.broadcast_to(facts[flag : flag + 1, 0:1], (8, 1))
        return jnp.where(flag > 0.5, corners[:, one : one + 1], corners[:, zero : zero + 1])

    made = []
    for side in range(2):
        flip = facts[side : side + 1, :]
        if side == 0:
            before = chosen(8 + 2, at_low, 1, 3)
            after = chosen(8 + 3, at_high, 0, 2)
        else:
            before = chosen(12 + 2, at_low, 4 + 3, 4 + 1)
            after = chosen(12 + 3, at_high, 4 + 2, 4 + 0)
        swap = jnp.broadcast_to(flip[:, 0:1], (8, 1)) > 0.5
        made.append(
            halo_row(
                kept[KEPT * side : KEPT * (side + 1), :],
                kept[2 * KEPT + 8 * side : 2 * KEPT + 8 * side + 8, :],
                below[8 * side : 8 * side + 8],
                above[8 * side : 8 * side + 8],
                jnp.where(swap, after, before),
                jnp.where(swap, before, after),
                flip,
                side == 0,
            )
        )
    return made


def first_kernel(
    facts, lower, upper, below_halo, above_halo, gifts, got, passed, outer, forcing, viscosity,
    flow, new_lower, new_upper, col_given, col_own, kept, cols,
):
    size = facts.shape[1]
    core = core_index()
    high, low = in_order(passed[1 - core], got[ROW_MESSAGE:, :])
    messages = (low, high)
    for side, message in enumerate(messages):
        kept[KEPT * side : KEPT * (side + 1), :] = turned(
            message[:KEPT], facts[side : side + 1, :]
        )
        edge = (size - 1) * side
        for layer, state in enumerate((lower, upper)):
            for k in range(4):
                at = 2 * KEPT + 8 * side + 4 * layer + k
                kept[at : at + 1, :] = state[k * size + edge : k * size + edge + 1, :]
    edges = [kept[KEPT * side : KEPT * side + 8, :] for side in range(2)]
    sides = in_order(gifts[1 - core, ROW_MESSAGE:], outer[...])
    rims = (*edges, columns_of(facts, *sides, cols))
    state = planes_of(lower, upper)
    outs = (new_lower, new_upper)
    for layer, out in enumerate(outs):
        new = moved(
            layer, state, below_halo, above_halo, forcing,
            stiffness_of(viscosity, facts, layer), rims,
        )
        for k in range(3):
            out[k * size : (k + 1) * size, :] = new[k]
        for side in range(2):
            out[4 * size + 8 * side : 4 * size + 8 * side + 8, :] = edges[side]
    for layer, out in enumerate(outs):
        out[3 * size : 4 * size, :] = warmed(layer, state, below_halo, above_halo, flow, rims)
    low, high = edge_columns([plane_of(ref, k) for ref in outs for k in range(4)], cols)
    corners = [message[CORNERS] for message in messages]
    corners = jnp.where(lanes(corners[0].shape) < 4, corners[0], shifted(corners[1], 4, 1))
    col_given[:8, :], col_own[:8, :] = in_order(high, low)[::-1]
    col_given[8:, :] = corners
    col_own[8:, :] = corners


def last_kernel(
    facts, lower, upper, below_halo, above_halo, gifts, outer, kept, forcing, viscosity, stress,
    flow, new_velocity, new_heat, partial, velocity, heat, cols, sems,
):
    sides = in_order(gifts[1 - core_index()], outer[...])
    edges = halo_rows(facts, kept, below_halo, above_halo, *sides)
    rims = (*edges, columns_of(facts, *sides, cols))
    state = planes_of(lower, upper)
    copies = []

    def send(source, target):
        copies.append(pltpu.make_async_copy(source, target, sems.at[len(copies)]))
        copies[-1].start()

    for layer in range(2):
        heat[layer] = warmed(layer, state, below_halo, above_halo, flow, rims)
        send(heat.at[layer], new_heat.at[layer])
    for layer in range(2):
        stiffness = stiffness_of(viscosity, facts, layer)
        new = moved(layer, state, below_halo, above_halo, forcing, stiffness, rims)
        for k in range(3):
            velocity[k, layer] = new[k]
            send(velocity.at[k, layer], new_velocity.at[k, layer])
    shares = [
        stiffness_of(viscosity, facts, layer)
        * sum(velocity[k, layer] * stress[k, layer] for k in range(3))
        for layer in range(2)
    ]
    partial[...] = (shares[0] + shares[1]) * (1.0 / 96.0)
    for copy in copies:
        copy.wait()


VMEM = pl.BlockSpec(memory_space=pltpu.VMEM)
FAR = pl.BlockSpec(memory_space=pltpu.HBM)


def call(kernel, outs, near, far=(), scratch=(), out_specs=None, flops=0):
    far = [pltpu.with_memory_space_constraint(a, pltpu.HBM) for a in far]
    arrays = (*near, *far)
    moved_bytes = 4 * sum(a.size for a in arrays)
    return pl.pallas_call(
        kernel,
        out_shape=[jax.ShapeDtypeStruct(shape, jnp.float32) for shape in outs],
        in_specs=[VMEM] * len(near) + [FAR] * len(far),
        out_specs=out_specs or [VMEM] * len(outs),
        scratch_shapes=list(scratch),
        compiler_params=pltpu.CompilerParams(vmem_limit_bytes=VMEM_BYTES),
        cost_estimate=pl.CostEstimate(
            flops=flops, bytes_accessed=moved_bytes, transcendentals=0
        ),
    )(*arrays)


def over_tiles(array, to):
    count = lax.axis_size("cap")
    return lax.ppermute(array, "cap", [(i, to(i) % count) for i in range(count)])


def of_chip(array):
    count = lax.axis_size("cap")
    pairs = [[i, i + 1] for i in range(0, count, 2)]
    return lax.all_gather(array, "cap", axis_index_groups=pairs)


def to_outer(array):
    return over_tiles(array, lambda i: i + 1 if i % 2 else i - 1)


def along(array, by):
    count = lax.axis_size("rad")
    return lax.ppermute(
        array, "rad", [(i, i + by) for i in range(count) if 0 <= i + by < count]
    )


def radial(lower, upper):
    return along(upper, 1), along(lower, -1)


def shards(
    adjoint_velocity, adjoint_heat, forcing, flow_velocity, forward_stress, viscosity, layer_mask,
    face_flips,
):
    size = adjoint_velocity.shape[-1]
    quarter = lax.axis_size("cap") // 4
    velocity, heat = adjoint_velocity[:, :, 0], adjoint_heat[:, 0]
    forces, flow, stress, visc = (
        forcing[:, :, 0], flow_velocity[:, :, 0], forward_stress[:, :, 0], viscosity[:, 0]
    )
    flips = face_flips.T
    f32 = jnp.float32
    lower, upper, row_own, gift, col_own, facts = call(
        pack_kernel,
        [(4 * size, size)] * 2
        + [(ROW_MESSAGE, size), (ROW_MESSAGE + 8, size), (8, size), (16, size)],
        (),
        (velocity, heat, layer_mask, flips, forces, flow, visc),
        (
            pltpu.SMEM(layer_mask.shape, jnp.int32),
            pltpu.VMEM(flips.shape, jnp.int32),
            pltpu.VMEM((2, 3, 2, 8, size), f32),
            pltpu.VMEM((2, 3, 2, 8, size), f32),
            pltpu.VMEM((2, 2, 8, size), f32),
            pltpu.VMEM((2, ROW_MESSAGE, size), f32),
            pltpu.VMEM((16, size), f32),
            pltpu.SemaphoreType.DMA((10,)),
            pltpu.SemaphoreType.DMA((6,)),
        ),
    )
    halos = radial(lower, upper)
    gifts = of_chip(gift)
    core = lax.rem(lax.axis_index("cap"), 2)
    given = lax.dynamic_index_in_dim(gifts, 1 - core, 0, keepdims=False)[:ROW_MESSAGE]
    got = over_tiles(
        jnp.concatenate([row_own, given]),
        lambda i: i - quarter - 1 if i % 2 else i + quarter + 1,
    )
    outer = to_outer(col_own)
    passed = of_chip(got[:ROW_MESSAGE])
    lower, upper, col_given, col_own, kept = call(
        first_kernel,
        [(4 * size + 16, size)] * 2 + [(16, size)] * 2 + [(2 * KEPT + 16, size)],
        (facts, lower, upper, *halos, gifts, got, passed, outer, forces, visc, flow),
        (),
        (pltpu.VMEM((16, size), f32),),
    )
    halos = radial(lower, upper)
    gifts = of_chip(col_given)
    outer = to_outer(col_own)
    new_velocity, new_heat, partial = call(
        last_kernel,
        [velocity.shape, heat.shape, (size, size)],
        (facts, lower, upper, *halos, gifts, outer, kept, forces, visc, stress, flow),
        (),
        (
            pltpu.VMEM(velocity.shape, f32),
            pltpu.VMEM(heat.shape, f32),
            pltpu.VMEM((16, size), f32),
            pltpu.SemaphoreType.DMA((8,)),
        ),
        [FAR, FAR, VMEM],
    )
    pieces = lax.all_to_all(partial, "rad", 0, 0, tiled=True)
    count = lax.axis_size("rad")
    gradient = jnp.sum(pieces.reshape(count, size // count, size), axis=0)
    return new_velocity[:, :, None], new_heat[:, None], gradient[None]


def solution(mesh):
    fields = P(None, "rad", "cap", None, None)
    scalar_field = P("rad", "cap", None, None)
    return jax.shard_map(
        shards,
        mesh=mesh,
        in_specs=(
            fields, scalar_field, fields, fields, fields, scalar_field, P("rad"), P(),
        ),
        out_specs=(fields, scalar_field, P("cap", "rad", None)),
        check_vma=False,
    )
```

```python
import jax
import jax.numpy as jnp
from jax import lax
from jax.experimental import pallas as pl
from jax.experimental.pallas import tpu as pltpu
from jax.sharding import PartitionSpec as P

RELAX = 0.8
STEP = 0.1
VMEM_BYTES = 24 * 1024 * 1024


def lanes(shape):
    return lax.broadcasted_iota(jnp.int32, shape, len(shape) - 1)


def rows(shape):
    return lax.broadcasted_iota(jnp.int32, shape, len(shape) - 2)


def shifted(plane, by, axis):
    return pltpu.roll(plane, by % plane.shape[axis], axis)


def plane_of(ref, k):
    size = ref.shape[1]
    return ref[k * size : (k + 1) * size, :]


EDGE, SECOND, STIFF, FORCE, FLOW, CORNERS = (slice(8 * n, 8 * n + 8) for n in range(6))
MESSAGE = 48
KEPT = 40


def core_index():
    return lax.rem(lax.axis_index("cap"), 2)


def in_order(from_partner, from_outside):
    second = core_index() == 1
    return (
        jnp.where(second, from_partner, from_outside),
        jnp.where(second, from_outside, from_partner),
    )


def pack_kernel(
    velocity, heat, mask, flips, forcing, flow, viscosity,
    lower, upper, row_own, gift, col_own, own_cols, facts,
    mask_here, flips_here, forcing_here, flow_here, viscosity_here, messages, cols, sems,
):
    size = lower.shape[1]
    copies = [
        pltpu.make_async_copy(mask, mask_here, sems.at[0]),
        pltpu.make_async_copy(flips, flips_here, sems.at[1]),
        pltpu.make_async_copy(forcing, forcing_here, sems.at[2]),
        pltpu.make_async_copy(flow, flow_here, sems.at[3]),
        pltpu.make_async_copy(viscosity, viscosity_here, sems.at[4]),
    ]
    for layer, out in enumerate((lower, upper)):
        for k in range(4):
            copies.append(
                pltpu.make_async_copy(
                    velocity.at[k, layer] if k < 3 else heat.at[layer],
                    out.at[pl.ds(k * size, size)],
                    sems.at[5 + 4 * layer + k],
                )
            )
    for copy in copies[5:] + copies[:5]:
        copy.start()
    for copy in copies:
        copy.wait()

    width = facts.shape[1]
    tiles = lax.axis_size("cap")
    tile = lax.axis_index("cap")
    bits = flips_here[...]

    def bits_of(at):
        picked = jnp.where(lanes(bits.shape) == lax.rem(at + tiles, tiles), bits, 0)
        return jnp.sum(picked.astype(jnp.float32), axis=1, keepdims=True)

    facts[0:4, :] = jnp.broadcast_to(bits_of(tile), (4, width))
    facts[8:12, :] = jnp.broadcast_to(bits_of(tile - 1), (4, width))
    facts[12:16, :] = jnp.broadcast_to(bits_of(tile + 1), (4, width))
    for layer in range(2):
        scale = 1.0 + 4.0 * mask_here[layer].astype(jnp.float32)
        facts[4 + layer : 5 + layer, :] = jnp.full((1, width), scale, jnp.float32)

    planes = [plane_of(ref, k) for ref in (lower, upper) for k in range(4)]
    given = [viscosity_here[layer] for layer in range(2)]
    given += [forcing_here[k, layer] for layer in range(2) for k in range(3)]
    given += [flow_here[k, layer] for layer in range(2) for k in range(3)]
    lane = lanes(planes[0].shape)
    gathered = jnp.zeros(planes[0].shape, jnp.float32)
    for k, plane in enumerate(planes):
        gathered = jnp.where((lane >> 2) == k, shifted(plane, 4 * k + 2, 1), gathered)
    for m, plane in enumerate(given):
        gathered = jnp.where((lane >> 1) == 16 + m, shifted(plane, 33 + 2 * m, 1), gathered)
    cols[...] = gathered.T[:64]
    lane = lanes((8, size))
    ends = []
    for edge, row in ((0, 0), (0, size - 1)):
        ends.append([plane[row : row + 1, :] for plane in planes])
    first, last = (jnp.concatenate(end, 0) for end in ends)
    corners = jnp.where(
        lane < 2,
        jnp.where(lane == 0, first, shifted(first, 2, 1)),
        jnp.where(lane == 2, shifted(last, 2, 1), shifted(last, 4, 1)),
    )
    none = jnp.zeros((1, size), jnp.float32)
    for side, (edge, second) in enumerate(((2, 3), (1, 0))):
        out = messages.at[side]
        out[EDGE, :] = cols[pl.ds(edge, 8, stride=4), :]
        out[SECOND, :] = cols[pl.ds(second, 8, stride=4), :]
        out[CORNERS, :] = corners
        own_cols[8 * side : 8 * side + 8, :] = out[EDGE, :]
        start = 33 - side
        for layer in range(2):
            at = 4 * layer
            stiff = cols[start + 2 * layer : start + 2 * layer + 1, :]
            stiff = stiff * facts[4 + layer : 5 + layer, :]
            force = start + 4 + 6 * layer
            carry = start + 16 + 6 * layer
            for k in range(3):
                out[16 + at + k : 17 + at + k, :] = stiff
                out[24 + at + k : 25 + at + k, :] = cols[force + 2 * k : force + 2 * k + 1, :]
                out[32 + at + k : 33 + at + k, :] = none
            out[19 + at : 20 + at, :] = cols[carry + 2 : carry + 3, :]
            out[27 + at : 28 + at, :] = cols[carry : carry + 1, :]
            out[35 + at : 36 + at, :] = cols[carry + 4 : carry + 5, :]
    gift[:8, :], row_own[...] = in_order(first, last)[::-1]
    core = core_index()
    gift[8:, :] = messages[1 - core]
    col_own[...] = messages[core]


def turned(rim, flip):
    lane = lanes(rim.shape)
    picks = jnp.where(jnp.broadcast_to(flip, rim.shape) > 0.5, rim.shape[1] - 1 - lane, lane)
    return jnp.take_along_axis(rim, picks, axis=1)


def columns_of(low, high, cols):
    cols[pl.ds(0, 8, stride=2), :] = high
    cols[pl.ds(1, 8, stride=2), :] = low
    size = low.shape[1]
    rest = jnp.zeros((size - 16, size), jnp.float32)
    return jnp.concatenate([cols[...], rest], 0).T


def lateral(plane, k, rims):
    low_row, high_row, columns = rims
    size = plane.shape[0]
    ends = shifted(columns, -(2 * k + 1), 1)
    row, lane = rows(plane.shape), lanes(plane.shape)
    above = jnp.where(row == 0, low_row[k : k + 1, :], shifted(plane, 1, 0))
    below = jnp.where(row == size - 1, high_row[k : k + 1, :], shifted(plane, -1, 0))
    left = jnp.where(lane == 0, ends, shifted(plane, 1, 1))
    right = jnp.where(lane == size - 1, ends, shifted(plane, -1, 1))
    return above, below, left, right


def neighbours(layer, k, state, below_halo, above_halo, rims):
    under = plane_of(below_halo, k) if layer == 0 else state[0][k]
    over = plane_of(above_halo, k) if layer == 1 else state[1][k]
    return (*lateral(state[layer][k], layer * 4 + k, rims), under, over)


def moved(layer, state, below_halo, above_halo, forcing, stiffness, rims):
    new = []
    weight = RELAX / (6.0 * stiffness + 1.0)
    for k in range(3):
        plane = state[layer][k]
        total = sum(neighbours(layer, k, state, below_halo, above_halo, rims))
        image = stiffness * (6.0 * plane - total) + plane
        drive = forcing[k, layer]
        if k == 2:
            drive = drive + state[layer][3]
        new.append(plane + weight * (drive - image))
    return new


def warmed(layer, state, below_halo, above_halo, flow, rims):
    plane = state[layer][3]
    up, down, left, right, under, over = neighbours(
        layer, 3, state, below_halo, above_halo, rims
    )
    total = up + down + left + right + under + over
    carried = 0.5 * (
        flow[0, layer] * (down - up)
        + flow[1, layer] * (right - left)
        + flow[2, layer] * (over - under)
    )
    return plane + STEP * (total - 6.0 * plane + carried + state[layer][2])


def stiffness_of(viscosity, facts, layer):
    return viscosity[layer] * facts[4 + layer : 5 + layer, :]


def planes_of(lower, upper):
    return [[plane_of(ref, k) for k in range(4)] for ref in (lower, upper)]


def halo_row(message, own, below, above, left_end, right_end, flip, low):
    edge, second = message[EDGE], message[SECOND]
    lane, row = lanes(edge.shape), rows(edge.shape)
    left = jnp.where(lane == 0, left_end, shifted(edge, 1, 1))
    right = jnp.where(lane == edge.shape[1] - 1, right_end, shifted(edge, -1, 1))
    other = shifted(edge, 4, 0)
    under = jnp.where(row < 4, shifted(below, 4, 0), other)
    over = jnp.where(row < 4, other, shifted(above, 4, 0))
    total = own + second + left + right + under + over
    stiffness = message[STIFF]
    image = stiffness * (6.0 * edge - total) + edge
    field = row % 4
    drive = message[FORCE] + jnp.where(field == 2, shifted(edge, -1, 0), 0.0)
    velocity = edge + (RELAX / (6.0 * stiffness + 1.0)) * (drive - image)
    step_i = own - second if low else second - own
    step_j = (right - left) * (1.0 - 2.0 * flip)
    carried = 0.5 * (
        message[STIFF] * step_i + message[FORCE] * step_j + message[FLOW] * (over - under)
    )
    heat = edge + STEP * (total - 6.0 * edge + carried + shifted(edge, 1, 0))
    return jnp.where(field == 3, heat, velocity)


def halo_columns(facts, kept, own_cols, below_halo, above_halo, from_low_row, from_high_row):
    size = facts.shape[1]
    below, above = below_halo[4 * size :, :], above_halo[4 * size :, :]
    at_low, at_high = from_low_row[8:16, :], from_high_row[8:16, :]

    def chosen(flag, corners, one, zero):
        flag = jnp.broadcast_to(facts[flag : flag + 1, 0:1], (8, 1))
        return jnp.where(flag > 0.5, corners[:, one : one + 1], corners[:, zero : zero + 1])

    made = []
    for side in range(2):
        flip = facts[2 + side : 3 + side, :]
        if side == 0:
            before = chosen(8, at_low, 2, 3)
            after = chosen(8 + 1, at_high, 0, 1)
        else:
            before = chosen(12, at_low, 4 + 3, 4 + 2)
            after = chosen(12 + 1, at_high, 4 + 1, 4 + 0)
        swap = jnp.broadcast_to(flip[:, 0:1], (8, 1)) > 0.5
        made.append(
            halo_row(
                kept[KEPT * side : KEPT * (side + 1), :],
                own_cols[8 * side : 8 * side + 8, :],
                below[8 * side : 8 * side + 8],
                above[8 * side : 8 * side + 8],
                jnp.where(swap, after, before),
                jnp.where(swap, before, after),
                flip,
                side == 0,
            )
        )
    return made


def first_kernel(
    facts, lower, upper, below_halo, above_halo, gifts, got, passed, outer, forcing, viscosity,
    flow, new_lower, new_upper, row_low, row_high, kept, cols,
):
    size = facts.shape[1]
    core = core_index()
    high, low = in_order(passed[1 - core], got[8:16, :])
    row_rims = turned(low, facts[0:1, :]), turned(high, facts[1:2, :])
    messages = in_order(gifts[1 - core, 8:], outer[...])
    for side, message in enumerate(messages):
        kept[KEPT * side : KEPT * (side + 1), :] = turned(
            message[:KEPT], facts[2 + side : 3 + side, :]
        )
    edges = [kept[KEPT * side : KEPT * side + 8, :] for side in range(2)]
    rims = (*row_rims, columns_of(*edges, cols))
    state = planes_of(lower, upper)
    outs = (new_lower, new_upper)
    for layer, out in enumerate(outs):
        new = moved(
            layer, state, below_halo, above_halo, forcing,
            stiffness_of(viscosity, facts, layer), rims,
        )
        for k in range(3):
            out[k * size : (k + 1) * size, :] = new[k]
        for side in range(2):
            out[4 * size + 8 * side : 4 * size + 8 * side + 8, :] = edges[side]
    for layer, out in enumerate(outs):
        out[3 * size : 4 * size, :] = warmed(layer, state, below_halo, above_halo, flow, rims)
    corners = [message[CORNERS] for message in messages]
    corners = jnp.where(lanes(corners[0].shape) < 4, corners[0], shifted(corners[1], 4, 1))
    for message, edge in ((row_low, 0), (row_high, size - 1)):
        message[8:, :] = corners
        for layer, out in enumerate(outs):
            for k in range(4):
                at = 4 * layer + k
                message[at : at + 1, :] = out[k * size + edge : k * size + edge + 1, :]


def last_velocity_kernel(
    facts, lower, upper, below_halo, above_halo, lr, hr, kept, own_cols, forcing, viscosity,
    stress, new_velocity, partial, edge_rows, columns, cols,
):
    edge_rows[0:8, :] = turned(lr[0:8, :], facts[0:1, :])
    edge_rows[8:16, :] = turned(hr[0:8, :], facts[1:2, :])
    made = halo_columns(facts, kept, own_cols, below_halo, above_halo, lr, hr)
    columns[...] = columns_of(*made, cols)
    rims = (edge_rows[0:8, :], edge_rows[8:16, :], columns[...])
    state = planes_of(lower, upper)
    for layer in range(2):
        stiffness = stiffness_of(viscosity, facts, layer)
        new = moved(layer, state, below_halo, above_halo, forcing, stiffness, rims)
        for k in range(3):
            new_velocity[k, layer] = new[k]
        share = stiffness * sum(new[k] * stress[k, layer] for k in range(3))
        partial[...] = share if layer == 0 else (partial[...] + share) * (1.0 / 96.0)


def last_heat_kernel(
    lower, upper, below_halo, above_halo, edge_rows, columns, flow, velocity_near,
    new_velocity, new_heat, heat, sems,
):
    copies = []

    def send(source, target):
        copies.append(pltpu.make_async_copy(source, target, sems.at[len(copies)]))
        copies[-1].start()

    send(velocity_near, new_velocity)
    rims = (edge_rows[0:8, :], edge_rows[8:16, :], columns[...])
    state = planes_of(lower, upper)
    for layer in range(2):
        heat[layer] = warmed(layer, state, below_halo, above_halo, flow, rims)
        send(heat.at[layer], new_heat.at[layer])
    for copy in copies:
        copy.wait()


VMEM = pl.BlockSpec(memory_space=pltpu.VMEM)
FAR = pl.BlockSpec(memory_space=pltpu.HBM)


def call(kernel, outs, near, far=(), scratch=(), out_specs=None, flops=0):
    far = [pltpu.with_memory_space_constraint(a, pltpu.HBM) for a in far]
    arrays = (*near, *far)
    moved_bytes = 4 * sum(a.size for a in arrays)
    return pl.pallas_call(
        kernel,
        out_shape=[jax.ShapeDtypeStruct(shape, jnp.float32) for shape in outs],
        in_specs=[VMEM] * len(near) + [FAR] * len(far),
        out_specs=out_specs or [VMEM] * len(outs),
        scratch_shapes=list(scratch),
        compiler_params=pltpu.CompilerParams(vmem_limit_bytes=VMEM_BYTES),
        cost_estimate=pl.CostEstimate(
            flops=flops, bytes_accessed=moved_bytes, transcendentals=0
        ),
    )(*arrays)


def over_tiles(array, to):
    count = lax.axis_size("cap")
    return lax.ppermute(array, "cap", [(i, to(i) % count) for i in range(count)])


def of_chip(array):
    count = lax.axis_size("cap")
    pairs = [[i, i + 1] for i in range(0, count, 2)]
    return lax.all_gather(array, "cap", axis_index_groups=pairs)


def to_outer(array):
    return over_tiles(array, lambda i: i + 1 if i % 2 else i - 1)


def along(array, by):
    count = lax.axis_size("rad")
    return lax.ppermute(
        array, "rad", [(i, i + by) for i in range(count) if 0 <= i + by < count]
    )


def radial(lower, upper):
    return along(upper, 1), along(lower, -1)


def shards(
    adjoint_velocity, adjoint_heat, forcing, flow_velocity, forward_stress, viscosity, layer_mask,
    face_flips,
):
    size = adjoint_velocity.shape[-1]
    quarter = lax.axis_size("cap") // 4
    velocity, heat = adjoint_velocity[:, :, 0], adjoint_heat[:, 0]
    forces, flow, stress, visc = (
        forcing[:, :, 0], flow_velocity[:, :, 0], forward_stress[:, :, 0], viscosity[:, 0]
    )
    flips = face_flips.T
    f32 = jnp.float32
    lower, upper, row_own, gift, col_own, own_cols, facts = call(
        pack_kernel,
        [(4 * size, size)] * 2
        + [(8, size), (MESSAGE + 8, size), (MESSAGE, size), (16, size), (16, size)],
        (),
        (velocity, heat, layer_mask, flips, forces, flow, visc),
        (
            pltpu.SMEM(layer_mask.shape, jnp.int32),
            pltpu.VMEM(flips.shape, jnp.int32),
            pltpu.VMEM(forces.shape, f32),
            pltpu.VMEM(flow.shape, f32),
            pltpu.VMEM(visc.shape, f32),
            pltpu.VMEM((2, MESSAGE, size), f32),
            pltpu.VMEM((64, size), f32),
            pltpu.SemaphoreType.DMA((13,)),
        ),
    )
    halos = radial(lower, upper)
    gifts = of_chip(gift)
    core = lax.rem(lax.axis_index("cap"), 2)
    given = lax.dynamic_index_in_dim(gifts, 1 - core, 0, keepdims=False)[:8]
    got = over_tiles(
        jnp.concatenate([row_own, given]),
        lambda i: i - quarter - 1 if i % 2 else i + quarter + 1,
    )
    outer = to_outer(col_own)
    passed = of_chip(got[:8])
    lower, upper, row_low, row_high, kept = call(
        first_kernel,
        [(4 * size + 16, size)] * 2 + [(16, size)] * 2 + [(2 * KEPT, size)],
        (facts, lower, upper, *halos, gifts, got, passed, outer, forces, visc, flow),
        (),
        (pltpu.VMEM((16, size), f32),),
    )
    halos = radial(lower, upper)
    from_low_row = over_tiles(row_high, lambda i: i + quarter)
    from_high_row = over_tiles(row_low, lambda i: i - quarter)
    velocity_near, partial, edge_rows, columns = call(
        last_velocity_kernel,
        [velocity.shape, (size, size), (16, size), (size, size)],
        (
            facts, lower, upper, *halos, from_low_row, from_high_row, kept, own_cols, forces,
            visc, stress,
        ),
        (),
        (pltpu.VMEM((16, size), f32),),
    )
    pieces = lax.all_to_all(partial, "rad", 0, 0, tiled=True)
    new_velocity, new_heat = call(
        last_heat_kernel,
        [velocity.shape, heat.shape],
        (lower, upper, *halos, edge_rows, columns, flow, velocity_near),
        (),
        (pltpu.VMEM(heat.shape, f32), pltpu.SemaphoreType.DMA((3,))),
        [FAR, FAR],
    )
    pieces, new_heat = lax.optimization_barrier((pieces, new_heat))
    count = lax.axis_size("rad")
    gradient = jnp.sum(pieces.reshape(count, size // count, size), axis=0)
    return new_velocity[:, :, None], new_heat[:, None], gradient[None]


def solution(mesh):
    fields = P(None, "rad", "cap", None, None)
    scalar_field = P("rad", "cap", None, None)
    return jax.shard_map(
        shards,
        mesh=mesh,
        in_specs=(
            fields, scalar_field, fields, fields, fields, scalar_field, P("rad"), P(),
        ),
        out_specs=(fields, scalar_field, P("cap", "rad", None)),
        check_vma=False,
    )
```

```python
import jax
import jax.numpy as jnp
from jax import lax
from jax.experimental import pallas as pl
from jax.experimental.pallas import tpu as pltpu
from jax.sharding import PartitionSpec as P

RELAX = 0.8
STEP = 0.1
VMEM_BYTES = 24 * 1024 * 1024


def lanes(shape):
    return lax.broadcasted_iota(jnp.int32, shape, len(shape) - 1)


def rows(shape):
    return lax.broadcasted_iota(jnp.int32, shape, len(shape) - 2)


def shifted(plane, by, axis):
    return pltpu.roll(plane, by % plane.shape[axis], axis)


def evens(ref):
    return ref[pl.ds(0, 8, stride=2), :]


def odds(ref):
    return ref[pl.ds(1, 8, stride=2), :]


def edge_columns(planes, cols):
    shape = planes[0].shape
    half = lanes(shape) >> 1
    gathered = jnp.zeros(shape, jnp.float32)
    for k, plane in enumerate(planes):
        gathered = jnp.where(half == k, shifted(plane, 2 * k + 1, 1), gathered)
    cols[...] = gathered.T[:16]
    return odds(cols), evens(cols)


def plane_of(ref, k):
    size = ref.shape[1]
    return ref[k * size : (k + 1) * size, :]


EDGE, SECOND, STIFF, FORCE, FLOW, CORNERS = (slice(8 * n, 8 * n + 8) for n in range(6))
ROW_MESSAGE = 48
KEPT = 40


def core_index():
    return lax.rem(lax.axis_index("cap"), 2)


def in_order(from_partner, from_outside):
    second = core_index() == 1
    return (
        jnp.where(second, from_partner, from_outside),
        jnp.where(second, from_outside, from_partner),
    )


def pack_kernel(
    velocity, heat, mask, flips, forcing, flow, viscosity,
    lower, upper, row_own, gift, col_own, facts,
    mask_here, flips_here, forcing_rims, flow_rims, viscosity_rims, messages, cols, sems, rim_sem,
):
    size = lower.shape[1]
    row_low, row_high = messages.at[0], messages.at[1]
    core = core_index()
    copies = [
        pltpu.make_async_copy(mask, mask_here, sems.at[0]),
        pltpu.make_async_copy(flips, flips_here, sems.at[1]),
    ]
    for layer, out in enumerate((lower, upper)):
        for k in range(4):
            copies.append(
                pltpu.make_async_copy(
                    velocity.at[k, layer] if k < 3 else heat.at[layer],
                    out.at[pl.ds(k * size, size)],
                    sems.at[2 + 4 * layer + k],
                )
            )
    for side, start in enumerate((0, size - 8)):
        for n, (source, target) in enumerate(
            ((forcing, forcing_rims), (flow, flow_rims), (viscosity, viscosity_rims))
        ):
            here = (slice(None),) * (len(source.shape) - 2) + (pl.ds(start, 8),)
            copies.append(
                pltpu.make_async_copy(
                    source.at[here], target.at[side], rim_sem.at[3 * side + n]
                )
            )
    for copy in copies:
        copy.start()
    for copy in copies:
        copy.wait()

    width = facts.shape[1]
    tiles = lax.axis_size("cap")
    tile = lax.axis_index("cap")
    bits = flips_here[...]
    row = rows(bits.shape)

    def bits_of(at):
        picked = jnp.where(lanes(bits.shape) == lax.rem(at + tiles, tiles), bits, 0)
        return jnp.sum(picked.astype(jnp.float32), axis=1, keepdims=True)

    facts[0:4, :] = jnp.broadcast_to(bits_of(tile), (4, width))
    facts[8:12, :] = jnp.broadcast_to(bits_of(tile - tiles // 4), (4, width))
    facts[12:16, :] = jnp.broadcast_to(bits_of(tile + tiles // 4), (4, width))
    for layer in range(2):
        scale = 1.0 + 4.0 * mask_here[layer].astype(jnp.float32)
        facts[4 + layer : 5 + layer, :] = jnp.full((1, width), scale, jnp.float32)

    planes = [plane_of(ref, k) for ref in (lower, upper) for k in range(4)]
    for side, (out, edge, second, rim) in enumerate(
        ((row_low, 0, 1, 0), (row_high, size - 1, size - 2, 7))
    ):
        for layer in range(2):
            scale = facts[4 + layer : 5 + layer, :]
            for k in range(4):
                at = 4 * layer + k
                plane = planes[at]
                out[at : at + 1, :] = plane[edge : edge + 1, :]
                out[8 + at : 9 + at, :] = plane[second : second + 1, :]
                if k < 3:
                    stiff = viscosity_rims[side, layer, rim : rim + 1, :] * scale
                    force = forcing_rims[side, k, layer, rim : rim + 1, :]
                    carry = jnp.zeros((1, width), jnp.float32)
                else:
                    stiff = flow_rims[side, 0, layer, rim : rim + 1, :]
                    force = flow_rims[side, 1, layer, rim : rim + 1, :]
                    carry = flow_rims[side, 2, layer, rim : rim + 1, :]
                out[16 + at : 17 + at, :] = stiff
                out[24 + at : 25 + at, :] = force
                out[32 + at : 33 + at, :] = carry
    first, last = row_low[EDGE, :], row_high[EDGE, :]
    lane = lanes(first.shape)
    corners = jnp.where(
        lane < 2,
        jnp.where(lane == 0, first, shifted(first, 2, 1)),
        jnp.where(lane == 2, shifted(last, 2, 1), shifted(last, 4, 1)),
    )
    row_low[CORNERS, :] = corners
    row_high[CORNERS, :] = corners
    low, high = edge_columns(planes, cols)
    row_own[...] = messages[1 - core]
    gift[:ROW_MESSAGE, :] = messages[core]
    gift[ROW_MESSAGE:, :], col_own[...] = in_order(high, low)[::-1]


def turned(rim, flip):
    lane = lanes(rim.shape)
    picks = jnp.where(jnp.broadcast_to(flip, rim.shape) > 0.5, rim.shape[1] - 1 - lane, lane)
    return jnp.take_along_axis(rim, picks, axis=1)


def columns_of(facts, low, high, cols):
    cols[pl.ds(0, 8, stride=2), :] = turned(high[:8], facts[3:4, :])
    cols[pl.ds(1, 8, stride=2), :] = turned(low[:8], facts[2:3, :])
    size = facts.shape[1]
    rest = jnp.zeros((size - 16, size), jnp.float32)
    return jnp.concatenate([cols[...], rest], 0).T


def lateral(plane, k, rims):
    low_row, high_row, columns = rims
    size = plane.shape[0]
    ends = shifted(columns, -(2 * k + 1), 1)
    row, lane = rows(plane.shape), lanes(plane.shape)
    above = jnp.where(row == 0, low_row[k : k + 1, :], shifted(plane, 1, 0))
    below = jnp.where(row == size - 1, high_row[k : k + 1, :], shifted(plane, -1, 0))
    left = jnp.where(lane == 0, ends, shifted(plane, 1, 1))
    right = jnp.where(lane == size - 1, ends, shifted(plane, -1, 1))
    return above, below, left, right


def neighbours(layer, k, state, below_halo, above_halo, rims):
    under = plane_of(below_halo, k) if layer == 0 else state[0][k]
    over = plane_of(above_halo, k) if layer == 1 else state[1][k]
    return (*lateral(state[layer][k], layer * 4 + k, rims), under, over)


def moved(layer, state, below_halo, above_halo, forcing, stiffness, rims):
    new = []
    weight = RELAX / (6.0 * stiffness + 1.0)
    for k in range(3):
        plane = state[layer][k]
        total = sum(neighbours(layer, k, state, below_halo, above_halo, rims))
        image = stiffness * (6.0 * plane - total) + plane
        drive = forcing[k, layer]
        if k == 2:
            drive = drive + state[layer][3]
        new.append(plane + weight * (drive - image))
    return new


def warmed(layer, state, below_halo, above_halo, flow, rims):
    plane = state[layer][3]
    up, down, left, right, under, over = neighbours(
        layer, 3, state, below_halo, above_halo, rims
    )
    total = up + down + left + right + under + over
    carried = 0.5 * (
        flow[0, layer] * (down - up)
        + flow[1, layer] * (right - left)
        + flow[2, layer] * (over - under)
    )
    return plane + STEP * (total - 6.0 * plane + carried + state[layer][2])


def stiffness_of(viscosity, facts, layer):
    return viscosity[layer] * facts[4 + layer : 5 + layer, :]


def planes_of(lower, upper):
    return [[plane_of(ref, k) for k in range(4)] for ref in (lower, upper)]


def halo_row(message, own, below, above, left_end, right_end, flip, low):
    edge, second = message[EDGE], message[SECOND]
    lane, row = lanes(edge.shape), rows(edge.shape)
    left = jnp.where(lane == 0, left_end, shifted(edge, 1, 1))
    right = jnp.where(lane == edge.shape[1] - 1, right_end, shifted(edge, -1, 1))
    other = shifted(edge, 4, 0)
    under = jnp.where(row < 4, shifted(below, 4, 0), other)
    over = jnp.where(row < 4, other, shifted(above, 4, 0))
    total = own + second + left + right + under + over
    stiffness = message[STIFF]
    image = stiffness * (6.0 * edge - total) + edge
    field = row % 4
    drive = message[FORCE] + jnp.where(field == 2, shifted(edge, -1, 0), 0.0)
    velocity = edge + (RELAX / (6.0 * stiffness + 1.0)) * (drive - image)
    step_i = own - second if low else second - own
    step_j = (right - left) * (1.0 - 2.0 * flip)
    carried = 0.5 * (
        message[STIFF] * step_i + message[FORCE] * step_j + message[FLOW] * (over - under)
    )
    heat = edge + STEP * (total - 6.0 * edge + carried + shifted(edge, 1, 0))
    return jnp.where(field == 3, heat, velocity)


def halo_rows(facts, kept, below_halo, above_halo, low_col, high_col):
    size = facts.shape[1]
    below, above = below_halo[4 * size :, :], above_halo[4 * size :, :]
    at_low, at_high = low_col[8:16], high_col[8:16]

    def chosen(flag, corners, one, zero):
        flag = jnp.broadcast_to(facts[flag : flag + 1, 0:1], (8, 1))
        return jnp.where(flag > 0.5, corners[:, one : one + 1], corners[:, zero : zero + 1])

    made = []
    for side in range(2):
        flip = facts[side : side + 1, :]
        if side == 0:
            before = chosen(8 + 2, at_low, 1, 3)
            after = chosen(8 + 3, at_high, 0, 2)
        else:
            before = chosen(12 + 2, at_low, 4 + 3, 4 + 1)
            after = chosen(12 + 3, at_high, 4 + 2, 4 + 0)
        swap = jnp.broadcast_to(flip[:, 0:1], (8, 1)) > 0.5
        made.append(
            halo_row(
                kept[KEPT * side : KEPT * (side + 1), :],
                kept[2 * KEPT + 8 * side : 2 * KEPT + 8 * side + 8, :],
                below[8 * side : 8 * side + 8],
                above[8 * side : 8 * side + 8],
                jnp.where(swap, after, before),
                jnp.where(swap, before, after),
                flip,
                side == 0,
            )
        )
    return made


def first_kernel(
    facts, lower, upper, below_halo, above_halo, gifts, got, passed, outer, forcing, viscosity,
    flow, new_lower, new_upper, col_given, col_own, kept, cols,
):
    size = facts.shape[1]
    core = core_index()
    high, low = in_order(passed[1 - core], got[ROW_MESSAGE:, :])
    messages = (low, high)
    for side, message in enumerate(messages):
        kept[KEPT * side : KEPT * (side + 1), :] = turned(
            message[:KEPT], facts[side : side + 1, :]
        )
        edge = (size - 1) * side
        for layer, state in enumerate((lower, upper)):
            for k in range(4):
                at = 2 * KEPT + 8 * side + 4 * layer + k
                kept[at : at + 1, :] = state[k * size + edge : k * size + edge + 1, :]
    edges = [kept[KEPT * side : KEPT * side + 8, :] for side in range(2)]
    sides = in_order(gifts[1 - core, ROW_MESSAGE:], outer[...])
    rims = (*edges, columns_of(facts, *sides, cols))
    state = planes_of(lower, upper)
    outs = (new_lower, new_upper)
    for layer, out in enumerate(outs):
        new = moved(
            layer, state, below_halo, above_halo, forcing,
            stiffness_of(viscosity, facts, layer), rims,
        )
        for k in range(3):
            out[k * size : (k + 1) * size, :] = new[k]
        for side in range(2):
            out[4 * size + 8 * side : 4 * size + 8 * side + 8, :] = edges[side]
    for layer, out in enumerate(outs):
        out[3 * size : 4 * size, :] = warmed(layer, state, below_halo, above_halo, flow, rims)
    low, high = edge_columns([plane_of(ref, k) for ref in outs for k in range(4)], cols)
    corners = [message[CORNERS] for message in messages]
    corners = jnp.where(lanes(corners[0].shape) < 4, corners[0], shifted(corners[1], 4, 1))
    col_given[:8, :], col_own[:8, :] = in_order(high, low)[::-1]
    col_given[8:, :] = corners
    col_own[8:, :] = corners


def last_velocity_kernel(
    facts, lower, upper, below_halo, above_halo, gifts, outer, kept, forcing, viscosity, stress,
    new_velocity, partial, edge_rows, columns, cols,
):
    sides = in_order(gifts[1 - core_index()], outer[...])
    edges = halo_rows(facts, kept, below_halo, above_halo, *sides)
    for side in range(2):
        edge_rows[8 * side : 8 * side + 8, :] = edges[side]
    columns[...] = columns_of(facts, *sides, cols)
    rims = (*edges, columns[...])
    state = planes_of(lower, upper)
    for layer in range(2):
        stiffness = stiffness_of(viscosity, facts, layer)
        new = moved(layer, state, below_halo, above_halo, forcing, stiffness, rims)
        for k in range(3):
            new_velocity[k, layer] = new[k]
        share = stiffness * sum(new[k] * stress[k, layer] for k in range(3))
        partial[...] = share if layer == 0 else (partial[...] + share) * (1.0 / 96.0)


def last_heat_kernel(
    lower, upper, below_halo, above_halo, edge_rows, columns, flow, velocity_near,
    new_velocity, new_heat, heat, sems,
):
    copies = []

    def send(source, target):
        copies.append(pltpu.make_async_copy(source, target, sems.at[len(copies)]))
        copies[-1].start()

    send(velocity_near, new_velocity)
    rims = (edge_rows[0:8, :], edge_rows[8:16, :], columns[...])
    state = planes_of(lower, upper)
    for layer in range(2):
        heat[layer] = warmed(layer, state, below_halo, above_halo, flow, rims)
        send(heat.at[layer], new_heat.at[layer])
    for copy in copies:
        copy.wait()


VMEM = pl.BlockSpec(memory_space=pltpu.VMEM)
FAR = pl.BlockSpec(memory_space=pltpu.HBM)


def call(kernel, outs, near, far=(), scratch=(), out_specs=None, flops=0):
    far = [pltpu.with_memory_space_constraint(a, pltpu.HBM) for a in far]
    arrays = (*near, *far)
    moved_bytes = 4 * sum(a.size for a in arrays)
    return pl.pallas_call(
        kernel,
        out_shape=[jax.ShapeDtypeStruct(shape, jnp.float32) for shape in outs],
        in_specs=[VMEM] * len(near) + [FAR] * len(far),
        out_specs=out_specs or [VMEM] * len(outs),
        scratch_shapes=list(scratch),
        compiler_params=pltpu.CompilerParams(vmem_limit_bytes=VMEM_BYTES),
        cost_estimate=pl.CostEstimate(
            flops=flops, bytes_accessed=moved_bytes, transcendentals=0
        ),
    )(*arrays)


def over_tiles(array, to):
    count = lax.axis_size("cap")
    return lax.ppermute(array, "cap", [(i, to(i) % count) for i in range(count)])


def of_chip(array):
    count = lax.axis_size("cap")
    pairs = [[i, i + 1] for i in range(0, count, 2)]
    return lax.all_gather(array, "cap", axis_index_groups=pairs)


def to_outer(array):
    return over_tiles(array, lambda i: i + 1 if i % 2 else i - 1)


def along(array, by):
    count = lax.axis_size("rad")
    return lax.ppermute(
        array, "rad", [(i, i + by) for i in range(count) if 0 <= i + by < count]
    )


def radial(lower, upper):
    return along(upper, 1), along(lower, -1)


def shards(
    adjoint_velocity, adjoint_heat, forcing, flow_velocity, forward_stress, viscosity, layer_mask,
    face_flips,
):
    size = adjoint_velocity.shape[-1]
    quarter = lax.axis_size("cap") // 4
    velocity, heat = adjoint_velocity[:, :, 0], adjoint_heat[:, 0]
    forces, flow, stress, visc = (
        forcing[:, :, 0], flow_velocity[:, :, 0], forward_stress[:, :, 0], viscosity[:, 0]
    )
    flips = face_flips.T
    f32 = jnp.float32
    lower, upper, row_own, gift, col_own, facts = call(
        pack_kernel,
        [(4 * size, size)] * 2
        + [(ROW_MESSAGE, size), (ROW_MESSAGE + 8, size), (8, size), (16, size)],
        (),
        (velocity, heat, layer_mask, flips, forces, flow, visc),
        (
            pltpu.SMEM(layer_mask.shape, jnp.int32),
            pltpu.VMEM(flips.shape, jnp.int32),
            pltpu.VMEM((2, 3, 2, 8, size), f32),
            pltpu.VMEM((2, 3, 2, 8, size), f32),
            pltpu.VMEM((2, 2, 8, size), f32),
            pltpu.VMEM((2, ROW_MESSAGE, size), f32),
            pltpu.VMEM((16, size), f32),
            pltpu.SemaphoreType.DMA((10,)),
            pltpu.SemaphoreType.DMA((6,)),
        ),
    )
    halos = radial(lower, upper)
    gifts = of_chip(gift)
    core = lax.rem(lax.axis_index("cap"), 2)
    given = lax.dynamic_index_in_dim(gifts, 1 - core, 0, keepdims=False)[:ROW_MESSAGE]
    got = over_tiles(
        jnp.concatenate([row_own, given]),
        lambda i: i - quarter - 1 if i % 2 else i + quarter + 1,
    )
    outer = to_outer(col_own)
    passed = of_chip(got[:ROW_MESSAGE])
    lower, upper, col_given, col_own, kept = call(
        first_kernel,
        [(4 * size + 16, size)] * 2 + [(16, size)] * 2 + [(2 * KEPT + 16, size)],
        (facts, lower, upper, *halos, gifts, got, passed, outer, forces, visc, flow),
        (),
        (pltpu.VMEM((16, size), f32),),
    )
    halos = radial(lower, upper)
    gifts = of_chip(col_given)
    outer = to_outer(col_own)
    velocity_near, partial, edge_rows, columns = call(
        last_velocity_kernel,
        [velocity.shape, (size, size), (16, size), (size, size)],
        (facts, lower, upper, *halos, gifts, outer, kept, forces, visc, stress),
        (),
        (pltpu.VMEM((16, size), f32),),
    )
    pieces = lax.all_to_all(partial, "rad", 0, 0, tiled=True)
    new_velocity, new_heat = call(
        last_heat_kernel,
        [velocity.shape, heat.shape],
        (lower, upper, *halos, edge_rows, columns, flow, velocity_near),
        (),
        (pltpu.VMEM(heat.shape, f32), pltpu.SemaphoreType.DMA((3,))),
        [FAR, FAR],
    )
    pieces, new_heat = lax.optimization_barrier((pieces, new_heat))
    count = lax.axis_size("rad")
    gradient = jnp.sum(pieces.reshape(count, size // count, size), axis=0)
    return new_velocity[:, :, None], new_heat[:, None], gradient[None]


def solution(mesh):
    fields = P(None, "rad", "cap", None, None)
    scalar_field = P("rad", "cap", None, None)
    return jax.shard_map(
        shards,
        mesh=mesh,
        in_specs=(
            fields, scalar_field, fields, fields, fields, scalar_field, P("rad"), P(),
        ),
        out_specs=(fields, scalar_field, P("cap", "rad", None)),
        check_vma=False,
    )
```

```python
import jax
import jax.numpy as jnp
from jax import lax
from jax.experimental import pallas as pl
from jax.experimental.pallas import tpu as pltpu
from jax.sharding import PartitionSpec as P

RELAX = 0.8
STEP = 0.1
VMEM_BYTES = 24 * 1024 * 1024


def lanes(shape):
    return lax.broadcasted_iota(jnp.int32, shape, len(shape) - 1)


def rows(shape):
    return lax.broadcasted_iota(jnp.int32, shape, len(shape) - 2)


def shifted(plane, by, axis):
    return pltpu.roll(plane, by % plane.shape[axis], axis)


def evens(ref):
    return ref[pl.ds(0, 8, stride=2), :]


def odds(ref):
    return ref[pl.ds(1, 8, stride=2), :]


def edge_columns(planes, cols):
    shape = planes[0].shape
    half = lanes(shape) >> 1
    gathered = jnp.zeros(shape, jnp.float32)
    for k, plane in enumerate(planes):
        gathered = jnp.where(half == k, shifted(plane, 2 * k + 1, 1), gathered)
    cols[...] = gathered.T[:16]
    return odds(cols), evens(cols)


def plane_of(ref, k):
    size = ref.shape[1]
    return ref[k * size : (k + 1) * size, :]


EDGE, SECOND, STIFF, FORCE, FLOW, CORNERS = (slice(8 * n, 8 * n + 8) for n in range(6))
ROW_MESSAGE = 48
KEPT = 40


def core_index():
    return lax.rem(lax.axis_index("cap"), 2)


def in_order(from_partner, from_outside):
    second = core_index() == 1
    return (
        jnp.where(second, from_partner, from_outside),
        jnp.where(second, from_outside, from_partner),
    )


def pack_kernel(
    velocity, heat, mask, flips, forcing, flow, viscosity,
    lower, upper, row_own, gift, col_own, facts,
    mask_here, flips_here, forcing_rims, flow_rims, viscosity_rims, messages, cols, sems, rim_sem,
):
    size = lower.shape[1]
    row_low, row_high = messages.at[0], messages.at[1]
    core = core_index()
    copies = [
        pltpu.make_async_copy(mask, mask_here, sems.at[0]),
        pltpu.make_async_copy(flips, flips_here, sems.at[1]),
    ]
    for layer, out in enumerate((lower, upper)):
        for k in range(4):
            copies.append(
                pltpu.make_async_copy(
                    velocity.at[k, layer] if k < 3 else heat.at[layer],
                    out.at[pl.ds(k * size, size)],
                    sems.at[2 + 4 * layer + k],
                )
            )
    for side, start in enumerate((0, size - 8)):
        for n, (source, target) in enumerate(
            ((forcing, forcing_rims), (flow, flow_rims), (viscosity, viscosity_rims))
        ):
            here = (slice(None),) * (len(source.shape) - 2) + (pl.ds(start, 8),)
            copies.append(
                pltpu.make_async_copy(
                    source.at[here], target.at[side], rim_sem.at[3 * side + n]
                )
            )
    for copy in copies:
        copy.start()
    for copy in copies:
        copy.wait()

    width = facts.shape[1]
    tiles = lax.axis_size("cap")
    tile = lax.axis_index("cap")
    bits = flips_here[...]
    row = rows(bits.shape)

    def bits_of(at):
        picked = jnp.where(lanes(bits.shape) == lax.rem(at + tiles, tiles), bits, 0)
        return jnp.sum(picked.astype(jnp.float32), axis=1, keepdims=True)

    facts[0:4, :] = jnp.broadcast_to(bits_of(tile), (4, width))
    facts[8:12, :] = jnp.broadcast_to(bits_of(tile - tiles // 4), (4, width))
    facts[12:16, :] = jnp.broadcast_to(bits_of(tile + tiles // 4), (4, width))
    for layer in range(2):
        scale = 1.0 + 4.0 * mask_here[layer].astype(jnp.float32)
        facts[4 + layer : 5 + layer, :] = jnp.full((1, width), scale, jnp.float32)

    planes = [plane_of(ref, k) for ref in (lower, upper) for k in range(4)]
    for side, (out, edge, second, rim) in enumerate(
        ((row_low, 0, 1, 0), (row_high, size - 1, size - 2, 7))
    ):
        for layer in range(2):
            scale = facts[4 + layer : 5 + layer, :]
            for k in range(4):
                at = 4 * layer + k
                plane = planes[at]
                out[at : at + 1, :] = plane[edge : edge + 1, :]
                out[8 + at : 9 + at, :] = plane[second : second + 1, :]
                if k < 3:
                    stiff = viscosity_rims[side, layer, rim : rim + 1, :] * scale
                    force = forcing_rims[side, k, layer, rim : rim + 1, :]
                    carry = jnp.zeros((1, width), jnp.float32)
                else:
                    stiff = flow_rims[side, 0, layer, rim : rim + 1, :]
                    force = flow_rims[side, 1, layer, rim : rim + 1, :]
                    carry = flow_rims[side, 2, layer, rim : rim + 1, :]
                out[16 + at : 17 + at, :] = stiff
                out[24 + at : 25 + at, :] = force
                out[32 + at : 33 + at, :] = carry
    first, last = row_low[EDGE, :], row_high[EDGE, :]
    lane = lanes(first.shape)
    corners = jnp.where(
        lane < 2,
        jnp.where(lane == 0, first, shifted(first, 2, 1)),
        jnp.where(lane == 2, shifted(last, 2, 1), shifted(last, 4, 1)),
    )
    row_low[CORNERS, :] = corners
    row_high[CORNERS, :] = corners
    low, high = edge_columns(planes, cols)
    row_own[...] = messages[1 - core]
    gift[:ROW_MESSAGE, :] = messages[core]
    gift[ROW_MESSAGE:, :], col_own[...] = in_order(high, low)[::-1]


def turned(rim, flip):
    lane = lanes(rim.shape)
    picks = jnp.where(jnp.broadcast_to(flip, rim.shape) > 0.5, rim.shape[1] - 1 - lane, lane)
    return jnp.take_along_axis(rim, picks, axis=1)


def columns_of(facts, low, high, cols):
    cols[pl.ds(0, 8, stride=2), :] = turned(high[:8], facts[3:4, :])
    cols[pl.ds(1, 8, stride=2), :] = turned(low[:8], facts[2:3, :])
    size = facts.shape[1]
    rest = jnp.zeros((size - 16, size), jnp.float32)
    return jnp.concatenate([cols[...], rest], 0).T


def lateral(plane, k, rims):
    low_row, high_row, columns = rims
    size = plane.shape[0]
    ends = shifted(columns, -(2 * k + 1), 1)
    row, lane = rows(plane.shape), lanes(plane.shape)
    above = jnp.where(row == 0, low_row[k : k + 1, :], shifted(plane, 1, 0))
    below = jnp.where(row == size - 1, high_row[k : k + 1, :], shifted(plane, -1, 0))
    left = jnp.where(lane == 0, ends, shifted(plane, 1, 1))
    right = jnp.where(lane == size - 1, ends, shifted(plane, -1, 1))
    return above, below, left, right


def neighbours(layer, k, state, below_halo, above_halo, rims):
    under = plane_of(below_halo, k) if layer == 0 else state[0][k]
    over = plane_of(above_halo, k) if layer == 1 else state[1][k]
    return (*lateral(state[layer][k], layer * 4 + k, rims), under, over)


def moved(layer, state, below_halo, above_halo, forcing, stiffness, rims):
    new = []
    weight = RELAX / (6.0 * stiffness + 1.0)
    for k in range(3):
        plane = state[layer][k]
        total = sum(neighbours(layer, k, state, below_halo, above_halo, rims))
        image = stiffness * (6.0 * plane - total) + plane
        drive = forcing[k, layer]
        if k == 2:
            drive = drive + state[layer][3]
        new.append(plane + weight * (drive - image))
    return new


def warmed(layer, state, below_halo, above_halo, flow, rims):
    plane = state[layer][3]
    up, down, left, right, under, over = neighbours(
        layer, 3, state, below_halo, above_halo, rims
    )
    total = up + down + left + right + under + over
    carried = 0.5 * (
        flow[0, layer] * (down - up)
        + flow[1, layer] * (right - left)
        + flow[2, layer] * (over - under)
    )
    return plane + STEP * (total - 6.0 * plane + carried + state[layer][2])


def stiffness_of(viscosity, facts, layer):
    return viscosity[layer] * facts[4 + layer : 5 + layer, :]


def planes_of(lower, upper):
    return [[plane_of(ref, k) for k in range(4)] for ref in (lower, upper)]


def halo_row(message, own, below, above, left_end, right_end, flip, low):
    edge, second = message[EDGE], message[SECOND]
    lane, row = lanes(edge.shape), rows(edge.shape)
    left = jnp.where(lane == 0, left_end, shifted(edge, 1, 1))
    right = jnp.where(lane == edge.shape[1] - 1, right_end, shifted(edge, -1, 1))
    other = shifted(edge, 4, 0)
    under = jnp.where(row < 4, shifted(below, 4, 0), other)
    over = jnp.where(row < 4, other, shifted(above, 4, 0))
    total = own + second + left + right + under + over
    stiffness = message[STIFF]
    image = stiffness * (6.0 * edge - total) + edge
    field = row % 4
    drive = message[FORCE] + jnp.where(field == 2, shifted(edge, -1, 0), 0.0)
    velocity = edge + (RELAX / (6.0 * stiffness + 1.0)) * (drive - image)
    step_i = own - second if low else second - own
    step_j = (right - left) * (1.0 - 2.0 * flip)
    carried = 0.5 * (
        message[STIFF] * step_i + message[FORCE] * step_j + message[FLOW] * (over - under)
    )
    heat = edge + STEP * (total - 6.0 * edge + carried + shifted(edge, 1, 0))
    return jnp.where(field == 3, heat, velocity)


def halo_rows(facts, kept, below_halo, above_halo, low_col, high_col):
    size = facts.shape[1]
    below, above = below_halo[4 * size :, :], above_halo[4 * size :, :]
    at_low, at_high = low_col[8:16], high_col[8:16]

    def chosen(flag, corners, one, zero):
        flag = jnp.broadcast_to(facts[flag : flag + 1, 0:1], (8, 1))
        return jnp.where(flag > 0.5, corners[:, one : one + 1], corners[:, zero : zero + 1])

    made = []
    for side in range(2):
        flip = facts[side : side + 1, :]
        if side == 0:
            before = chosen(8 + 2, at_low, 1, 3)
            after = chosen(8 + 3, at_high, 0, 2)
        else:
            before = chosen(12 + 2, at_low, 4 + 3, 4 + 1)
            after = chosen(12 + 3, at_high, 4 + 2, 4 + 0)
        swap = jnp.broadcast_to(flip[:, 0:1], (8, 1)) > 0.5
        made.append(
            halo_row(
                kept[KEPT * side : KEPT * (side + 1), :],
                kept[2 * KEPT + 8 * side : 2 * KEPT + 8 * side + 8, :],
                below[8 * side : 8 * side + 8],
                above[8 * side : 8 * side + 8],
                jnp.where(swap, after, before),
                jnp.where(swap, before, after),
                flip,
                side == 0,
            )
        )
    return made


def cycle_layer(layer, out, facts, state, below_halo, above_halo, forcing, viscosity, flow, rims):
    size = facts.shape[1]
    new = moved(
        layer, state, below_halo, above_halo, forcing, stiffness_of(viscosity, facts, layer), rims
    )
    new.append(warmed(layer, state, below_halo, above_halo, flow, rims))
    for k in range(4):
        out[k * size : (k + 1) * size, :] = new[k]
    for side in range(2):
        out[4 * size + 8 * side : 4 * size + 8 * side + 8, :] = rims[side]


def first_upper_kernel(
    facts, lower, upper, above_halo, gifts, got, passed, outer, forcing, viscosity, flow,
    new_upper, kept, columns, cols,
):
    size = facts.shape[1]
    core = core_index()
    high, low = in_order(passed[1 - core], got[ROW_MESSAGE:, :])
    for side, message in enumerate((low, high)):
        kept[KEPT * side : KEPT * (side + 1), :] = turned(
            message[:KEPT], facts[side : side + 1, :]
        )
        kept[2 * KEPT + 16 + 8 * side : 2 * KEPT + 24 + 8 * side, :] = message[CORNERS]
    edges = [kept[KEPT * side : KEPT * side + 8, :] for side in range(2)]
    sides = in_order(gifts[1 - core, ROW_MESSAGE:], outer[...])
    columns[...] = columns_of(facts, *sides, cols)
    rims = (*edges, columns[...])
    cycle_layer(
        1, new_upper, facts, planes_of(lower, upper), None, above_halo, forcing, viscosity, flow,
        rims,
    )
    for side in range(2):
        edge = (size - 1) * side
        for layer, state in enumerate((lower, upper)):
            for k in range(4):
                at = 2 * KEPT + 8 * side + 4 * layer + k
                kept[at : at + 1, :] = state[k * size + edge : k * size + edge + 1, :]


def first_lower_kernel(
    facts, lower, upper, below_halo, kept, columns, new_upper, forcing, viscosity, flow,
    new_lower, col_given, col_own, cols,
):
    edges = [kept[KEPT * side : KEPT * side + 8, :] for side in range(2)]
    rims = (*edges, columns[...])
    cycle_layer(
        0, new_lower, facts, planes_of(lower, upper), below_halo, None, forcing, viscosity, flow,
        rims,
    )
    low, high = edge_columns([plane_of(ref, k) for ref in (new_lower, new_upper) for k in range(4)], cols)
    corners = [kept[2 * KEPT + 16 + 8 * side : 2 * KEPT + 24 + 8 * side, :] for side in range(2)]
    corners = jnp.where(lanes(corners[0].shape) < 4, corners[0], shifted(corners[1], 4, 1))
    col_given[:8, :], col_own[:8, :] = in_order(high, low)[::-1]
    col_given[8:, :] = corners
    col_own[8:, :] = corners


def last_velocity_kernel(
    facts, lower, upper, below_halo, above_halo, gifts, outer, kept, forcing, viscosity, stress,
    new_velocity, partial, edge_rows, columns, cols,
):
    sides = in_order(gifts[1 - core_index()], outer[...])
    edges = halo_rows(facts, kept, below_halo, above_halo, *sides)
    for side in range(2):
        edge_rows[8 * side : 8 * side + 8, :] = edges[side]
    columns[...] = columns_of(facts, *sides, cols)
    rims = (*edges, columns[...])
    state = planes_of(lower, upper)
    for layer in range(2):
        stiffness = stiffness_of(viscosity, facts, layer)
        new = moved(layer, state, below_halo, above_halo, forcing, stiffness, rims)
        for k in range(3):
            new_velocity[k, layer] = new[k]
        share = stiffness * sum(new[k] * stress[k, layer] for k in range(3))
        partial[...] = share if layer == 0 else (partial[...] + share) * (1.0 / 96.0)


def last_heat_kernel(
    lower, upper, below_halo, above_halo, edge_rows, columns, flow, velocity_near,
    new_velocity, new_heat, heat, sems,
):
    copies = []

    def send(source, target):
        copies.append(pltpu.make_async_copy(source, target, sems.at[len(copies)]))
        copies[-1].start()

    send(velocity_near, new_velocity)
    rims = (edge_rows[0:8, :], edge_rows[8:16, :], columns[...])
    state = planes_of(lower, upper)
    for layer in range(2):
        heat[layer] = warmed(layer, state, below_halo, above_halo, flow, rims)
        send(heat.at[layer], new_heat.at[layer])
    for copy in copies:
        copy.wait()


VMEM = pl.BlockSpec(memory_space=pltpu.VMEM)
FAR = pl.BlockSpec(memory_space=pltpu.HBM)


def call(kernel, outs, near, far=(), scratch=(), out_specs=None, flops=0):
    far = [pltpu.with_memory_space_constraint(a, pltpu.HBM) for a in far]
    arrays = (*near, *far)
    moved_bytes = 4 * sum(a.size for a in arrays)
    return pl.pallas_call(
        kernel,
        out_shape=[jax.ShapeDtypeStruct(shape, jnp.float32) for shape in outs],
        in_specs=[VMEM] * len(near) + [FAR] * len(far),
        out_specs=out_specs or [VMEM] * len(outs),
        scratch_shapes=list(scratch),
        compiler_params=pltpu.CompilerParams(vmem_limit_bytes=VMEM_BYTES),
        cost_estimate=pl.CostEstimate(
            flops=flops, bytes_accessed=moved_bytes, transcendentals=0
        ),
    )(*arrays)


def over_tiles(array, to):
    count = lax.axis_size("cap")
    return lax.ppermute(array, "cap", [(i, to(i) % count) for i in range(count)])


def of_chip(array):
    count = lax.axis_size("cap")
    pairs = [[i, i + 1] for i in range(0, count, 2)]
    return lax.all_gather(array, "cap", axis_index_groups=pairs)


def to_outer(array):
    return over_tiles(array, lambda i: i + 1 if i % 2 else i - 1)


def along(array, by):
    count = lax.axis_size("rad")
    return lax.ppermute(
        array, "rad", [(i, i + by) for i in range(count) if 0 <= i + by < count]
    )


def radial(lower, upper):
    return along(upper, 1), along(lower, -1)


def shards(
    adjoint_velocity, adjoint_heat, forcing, flow_velocity, forward_stress, viscosity, layer_mask,
    face_flips,
):
    size = adjoint_velocity.shape[-1]
    quarter = lax.axis_size("cap") // 4
    velocity, heat = adjoint_velocity[:, :, 0], adjoint_heat[:, 0]
    forces, flow, stress, visc = (
        forcing[:, :, 0], flow_velocity[:, :, 0], forward_stress[:, :, 0], viscosity[:, 0]
    )
    flips = face_flips.T
    f32 = jnp.float32
    lower, upper, row_own, gift, col_own, facts = call(
        pack_kernel,
        [(4 * size, size)] * 2
        + [(ROW_MESSAGE, size), (ROW_MESSAGE + 8, size), (8, size), (16, size)],
        (),
        (velocity, heat, layer_mask, flips, forces, flow, visc),
        (
            pltpu.SMEM(layer_mask.shape, jnp.int32),
            pltpu.VMEM(flips.shape, jnp.int32),
            pltpu.VMEM((2, 3, 2, 8, size), f32),
            pltpu.VMEM((2, 3, 2, 8, size), f32),
            pltpu.VMEM((2, 2, 8, size), f32),
            pltpu.VMEM((2, ROW_MESSAGE, size), f32),
            pltpu.VMEM((16, size), f32),
            pltpu.SemaphoreType.DMA((10,)),
            pltpu.SemaphoreType.DMA((6,)),
        ),
    )
    halos = radial(lower, upper)
    gifts = of_chip(gift)
    core = lax.rem(lax.axis_index("cap"), 2)
    given = lax.dynamic_index_in_dim(gifts, 1 - core, 0, keepdims=False)[:ROW_MESSAGE]
    got = over_tiles(
        jnp.concatenate([row_own, given]),
        lambda i: i - quarter - 1 if i % 2 else i + quarter + 1,
    )
    outer = to_outer(col_own)
    passed = of_chip(got[:ROW_MESSAGE])
    below_halo, above_halo = halos
    new_upper, kept, columns = call(
        first_upper_kernel,
        [(4 * size + 16, size), (2 * KEPT + 32, size), (size, size)],
        (facts, lower, upper, above_halo, gifts, got, passed, outer, forces, visc, flow),
        (),
        (pltpu.VMEM((16, size), f32),),
    )
    lower, col_given, col_own = call(
        first_lower_kernel,
        [(4 * size + 16, size), (16, size), (16, size)],
        (facts, lower, upper, below_halo, kept, columns, new_upper, forces, visc, flow),
        (),
        (pltpu.VMEM((16, size), f32),),
    )
    upper = new_upper
    halos = radial(lower, upper)
    gifts = of_chip(col_given)
    outer = to_outer(col_own)
    velocity_near, partial, edge_rows, columns = call(
        last_velocity_kernel,
        [velocity.shape, (size, size), (16, size), (size, size)],
        (facts, lower, upper, *halos, gifts, outer, kept, forces, visc, stress),
        (),
        (pltpu.VMEM((16, size), f32),),
    )
    pieces = lax.all_to_all(partial, "rad", 0, 0, tiled=True)
    new_velocity, new_heat = call(
        last_heat_kernel,
        [velocity.shape, heat.shape],
        (lower, upper, *halos, edge_rows, columns, flow, velocity_near),
        (),
        (pltpu.VMEM(heat.shape, f32), pltpu.SemaphoreType.DMA((3,))),
        [FAR, FAR],
    )
    pieces, new_heat = lax.optimization_barrier((pieces, new_heat))
    count = lax.axis_size("rad")
    gradient = jnp.sum(pieces.reshape(count, size // count, size), axis=0)
    return new_velocity[:, :, None], new_heat[:, None], gradient[None]


def solution(mesh):
    fields = P(None, "rad", "cap", None, None)
    scalar_field = P("rad", "cap", None, None)
    return jax.shard_map(
        shards,
        mesh=mesh,
        in_specs=(
            fields, scalar_field, fields, fields, fields, scalar_field, P("rad"), P(),
        ),
        out_specs=(fields, scalar_field, P("cap", "rad", None)),
        check_vma=False,
    )
```

```python
import jax
import jax.numpy as jnp
from jax import lax
from jax.experimental import pallas as pl
from jax.experimental.pallas import tpu as pltpu
from jax.sharding import PartitionSpec as P

RELAX = 0.8
STEP = 0.1
VMEM_BYTES = 24 * 1024 * 1024


def lanes(shape):
    return lax.broadcasted_iota(jnp.int32, shape, len(shape) - 1)


def rows(shape):
    return lax.broadcasted_iota(jnp.int32, shape, len(shape) - 2)


def shifted(plane, by, axis):
    return pltpu.roll(plane, by % plane.shape[axis], axis)


def evens(ref):
    return ref[pl.ds(0, 8, stride=2), :]


def odds(ref):
    return ref[pl.ds(1, 8, stride=2), :]


def edge_columns(planes, cols):
    shape = planes[0].shape
    half = lanes(shape) >> 1
    gathered = jnp.zeros(shape, jnp.float32)
    for k, plane in enumerate(planes):
        gathered = jnp.where(half == k, shifted(plane, 2 * k + 1, 1), gathered)
    cols[...] = gathered.T[:16]
    return odds(cols), evens(cols)


def plane_of(ref, k):
    size = ref.shape[1]
    return ref[k * size : (k + 1) * size, :]


EDGE, SECOND, STIFF, FORCE, FLOW, CORNERS = (slice(8 * n, 8 * n + 8) for n in range(6))
ROW_MESSAGE = 48
KEPT = 40


def core_index():
    return lax.rem(lax.axis_index("cap"), 2)


def in_order(from_partner, from_outside):
    second = core_index() == 1
    return (
        jnp.where(second, from_partner, from_outside),
        jnp.where(second, from_outside, from_partner),
    )


def pack_kernel(
    velocity, heat, mask, flips, forcing, flow, viscosity,
    lower, upper, row_own, gift, col_own, facts,
    mask_here, flips_here, forcing_rims, flow_rims, viscosity_rims, messages, cols, sems, rim_sem,
):
    size = lower.shape[1]
    row_low, row_high = messages.at[0], messages.at[1]
    core = core_index()
    planes_in = [
        pltpu.make_async_copy(
            velocity.at[k, layer] if k < 3 else heat.at[layer],
            out.at[pl.ds(k * size, size)],
            sems.at[2 + 4 * layer + k],
        )
        for layer, out in enumerate((lower, upper))
        for k in range(4)
    ]
    rims_in = [
        pltpu.make_async_copy(mask, mask_here, sems.at[0]),
        pltpu.make_async_copy(flips, flips_here, sems.at[1]),
    ]
    for side, start in enumerate((0, size - 8)):
        for n, (source, target) in enumerate(
            ((forcing, forcing_rims), (flow, flow_rims), (viscosity, viscosity_rims))
        ):
            here = (slice(None),) * (len(source.shape) - 2) + (pl.ds(start, 8),)
            rims_in.append(
                pltpu.make_async_copy(
                    source.at[here], target.at[side], rim_sem.at[3 * side + n]
                )
            )
    for copy in rims_in + planes_in:
        copy.start()
    for copy in rims_in:
        copy.wait()

    width = facts.shape[1]
    tiles = lax.axis_size("cap")
    tile = lax.axis_index("cap")
    bits = flips_here[...]
    row = rows(bits.shape)

    def bits_of(at):
        picked = jnp.where(lanes(bits.shape) == lax.rem(at + tiles, tiles), bits, 0)
        return jnp.sum(picked.astype(jnp.float32), axis=1, keepdims=True)

    facts[0:4, :] = jnp.broadcast_to(bits_of(tile), (4, width))
    facts[8:12, :] = jnp.broadcast_to(bits_of(tile - tiles // 4), (4, width))
    facts[12:16, :] = jnp.broadcast_to(bits_of(tile + tiles // 4), (4, width))
    for layer in range(2):
        scale = 1.0 + 4.0 * mask_here[layer].astype(jnp.float32)
        facts[4 + layer : 5 + layer, :] = jnp.full((1, width), scale, jnp.float32)

    for side, (out, rim) in enumerate(((row_low, 0), (row_high, 7))):
        for layer in range(2):
            scale = facts[4 + layer : 5 + layer, :]
            for k in range(4):
                at = 4 * layer + k
                if k < 3:
                    stiff = viscosity_rims[side, layer, rim : rim + 1, :] * scale
                    force = forcing_rims[side, k, layer, rim : rim + 1, :]
                    carry = jnp.zeros((1, width), jnp.float32)
                else:
                    stiff = flow_rims[side, 0, layer, rim : rim + 1, :]
                    force = flow_rims[side, 1, layer, rim : rim + 1, :]
                    carry = flow_rims[side, 2, layer, rim : rim + 1, :]
                out[16 + at : 17 + at, :] = stiff
                out[24 + at : 25 + at, :] = force
                out[32 + at : 33 + at, :] = carry
    for copy in planes_in:
        copy.wait()
    planes = [plane_of(ref, k) for ref in (lower, upper) for k in range(4)]
    for side, (out, edge, second, rim) in enumerate(
        ((row_low, 0, 1, 0), (row_high, size - 1, size - 2, 7))
    ):
        for layer in range(2):
            scale = facts[4 + layer : 5 + layer, :]
            for k in range(4):
                at = 4 * layer + k
                plane = planes[at]
                out[at : at + 1, :] = plane[edge : edge + 1, :]
                out[8 + at : 9 + at, :] = plane[second : second + 1, :]
    first, last = row_low[EDGE, :], row_high[EDGE, :]
    lane = lanes(first.shape)
    corners = jnp.where(
        lane < 2,
        jnp.where(lane == 0, first, shifted(first, 2, 1)),
        jnp.where(lane == 2, shifted(last, 2, 1), shifted(last, 4, 1)),
    )
    row_low[CORNERS, :] = corners
    row_high[CORNERS, :] = corners
    low, high = edge_columns(planes, cols)
    row_own[...] = messages[1 - core]
    gift[:ROW_MESSAGE, :] = messages[core]
    gift[ROW_MESSAGE:, :], col_own[...] = in_order(high, low)[::-1]


def turned(rim, flip):
    lane = lanes(rim.shape)
    picks = jnp.where(jnp.broadcast_to(flip, rim.shape) > 0.5, rim.shape[1] - 1 - lane, lane)
    return jnp.take_along_axis(rim, picks, axis=1)


def columns_of(facts, low, high, cols):
    cols[pl.ds(0, 8, stride=2), :] = turned(high[:8], facts[3:4, :])
    cols[pl.ds(1, 8, stride=2), :] = turned(low[:8], facts[2:3, :])
    size = facts.shape[1]
    rest = jnp.zeros((size - 16, size), jnp.float32)
    return jnp.concatenate([cols[...], rest], 0).T


def lateral(plane, k, rims):
    low_row, high_row, columns = rims
    size = plane.shape[0]
    ends = shifted(columns, -(2 * k + 1), 1)
    row, lane = rows(plane.shape), lanes(plane.shape)
    above = jnp.where(row == 0, low_row[k : k + 1, :], shifted(plane, 1, 0))
    below = jnp.where(row == size - 1, high_row[k : k + 1, :], shifted(plane, -1, 0))
    left = jnp.where(lane == 0, ends, shifted(plane, 1, 1))
    right = jnp.where(lane == size - 1, ends, shifted(plane, -1, 1))
    return above, below, left, right


def neighbours(layer, k, state, below_halo, above_halo, rims):
    under = plane_of(below_halo, k) if layer == 0 else state[0][k]
    over = plane_of(above_halo, k) if layer == 1 else state[1][k]
    return (*lateral(state[layer][k], layer * 4 + k, rims), under, over)


def moved(layer, state, below_halo, above_halo, forcing, stiffness, rims):
    new = []
    weight = RELAX / (6.0 * stiffness + 1.0)
    for k in range(3):
        plane = state[layer][k]
        total = sum(neighbours(layer, k, state, below_halo, above_halo, rims))
        image = stiffness * (6.0 * plane - total) + plane
        drive = forcing[k, layer]
        if k == 2:
            drive = drive + state[layer][3]
        new.append(plane + weight * (drive - image))
    return new


def warmed(layer, state, below_halo, above_halo, flow, rims):
    plane = state[layer][3]
    up, down, left, right, under, over = neighbours(
        layer, 3, state, below_halo, above_halo, rims
    )
    total = up + down + left + right + under + over
    carried = 0.5 * (
        flow[0, layer] * (down - up)
        + flow[1, layer] * (right - left)
        + flow[2, layer] * (over - under)
    )
    return plane + STEP * (total - 6.0 * plane + carried + state[layer][2])


def stiffness_of(viscosity, facts, layer):
    return viscosity[layer] * facts[4 + layer : 5 + layer, :]


def planes_of(lower, upper):
    return [[plane_of(ref, k) for k in range(4)] for ref in (lower, upper)]


def halo_row(message, own, below, above, left_end, right_end, flip, low):
    edge, second = message[EDGE], message[SECOND]
    lane, row = lanes(edge.shape), rows(edge.shape)
    left = jnp.where(lane == 0, left_end, shifted(edge, 1, 1))
    right = jnp.where(lane == edge.shape[1] - 1, right_end, shifted(edge, -1, 1))
    other = shifted(edge, 4, 0)
    under = jnp.where(row < 4, shifted(below, 4, 0), other)
    over = jnp.where(row < 4, other, shifted(above, 4, 0))
    total = own + second + left + right + under + over
    stiffness = message[STIFF]
    image = stiffness * (6.0 * edge - total) + edge
    field = row % 4
    drive = message[FORCE] + jnp.where(field == 2, shifted(edge, -1, 0), 0.0)
    velocity = edge + (RELAX / (6.0 * stiffness + 1.0)) * (drive - image)
    step_i = own - second if low else second - own
    step_j = (right - left) * (1.0 - 2.0 * flip)
    carried = 0.5 * (
        message[STIFF] * step_i + message[FORCE] * step_j + message[FLOW] * (over - under)
    )
    heat = edge + STEP * (total - 6.0 * edge + carried + shifted(edge, 1, 0))
    return jnp.where(field == 3, heat, velocity)


def halo_rows(facts, kept, below_halo, above_halo, low_col, high_col):
    size = facts.shape[1]
    below, above = below_halo[4 * size :, :], above_halo[4 * size :, :]
    at_low, at_high = low_col[8:16], high_col[8:16]

    def chosen(flag, corners, one, zero):
        flag = jnp.broadcast_to(facts[flag : flag + 1, 0:1], (8, 1))
        return jnp.where(flag > 0.5, corners[:, one : one + 1], corners[:, zero : zero + 1])

    made = []
    for side in range(2):
        flip = facts[side : side + 1, :]
        if side == 0:
            before = chosen(8 + 2, at_low, 1, 3)
            after = chosen(8 + 3, at_high, 0, 2)
        else:
            before = chosen(12 + 2, at_low, 4 + 3, 4 + 1)
            after = chosen(12 + 3, at_high, 4 + 2, 4 + 0)
        swap = jnp.broadcast_to(flip[:, 0:1], (8, 1)) > 0.5
        made.append(
            halo_row(
                kept[KEPT * side : KEPT * (side + 1), :],
                kept[2 * KEPT + 8 * side : 2 * KEPT + 8 * side + 8, :],
                below[8 * side : 8 * side + 8],
                above[8 * side : 8 * side + 8],
                jnp.where(swap, after, before),
                jnp.where(swap, before, after),
                flip,
                side == 0,
            )
        )
    return made


def first_kernel(
    facts, lower, upper, below_halo, above_halo, gifts, got, passed, outer, forcing, viscosity,
    flow, new_lower, new_upper, col_given, col_own, kept, cols,
):
    size = facts.shape[1]
    core = core_index()
    high, low = in_order(passed[1 - core], got[ROW_MESSAGE:, :])
    messages = (low, high)
    for side, message in enumerate(messages):
        kept[KEPT * side : KEPT * (side + 1), :] = turned(
            message[:KEPT], facts[side : side + 1, :]
        )
        edge = (size - 1) * side
        for layer, state in enumerate((lower, upper)):
            for k in range(4):
                at = 2 * KEPT + 8 * side + 4 * layer + k
                kept[at : at + 1, :] = state[k * size + edge : k * size + edge + 1, :]
    edges = [kept[KEPT * side : KEPT * side + 8, :] for side in range(2)]
    sides = in_order(gifts[1 - core, ROW_MESSAGE:], outer[...])
    rims = (*edges, columns_of(facts, *sides, cols))
    state = planes_of(lower, upper)
    outs = (new_lower, new_upper)
    for layer, out in enumerate(outs):
        new = moved(
            layer, state, below_halo, above_halo, forcing,
            stiffness_of(viscosity, facts, layer), rims,
        )
        for k in range(3):
            out[k * size : (k + 1) * size, :] = new[k]
        for side in range(2):
            out[4 * size + 8 * side : 4 * size + 8 * side + 8, :] = edges[side]
    for layer, out in enumerate(outs):
        out[3 * size : 4 * size, :] = warmed(layer, state, below_halo, above_halo, flow, rims)
    low, high = edge_columns([plane_of(ref, k) for ref in outs for k in range(4)], cols)
    corners = [message[CORNERS] for message in messages]
    corners = jnp.where(lanes(corners[0].shape) < 4, corners[0], shifted(corners[1], 4, 1))
    col_given[:8, :], col_own[:8, :] = in_order(high, low)[::-1]
    col_given[8:, :] = corners
    col_own[8:, :] = corners


def last_velocity_kernel(
    facts, lower, upper, below_halo, above_halo, gifts, outer, kept, forcing, viscosity, stress,
    new_velocity, partial, edge_rows, columns, cols,
):
    sides = in_order(gifts[1 - core_index()], outer[...])
    edges = halo_rows(facts, kept, below_halo, above_halo, *sides)
    for side in range(2):
        edge_rows[8 * side : 8 * side + 8, :] = edges[side]
    columns[...] = columns_of(facts, *sides, cols)
    rims = (*edges, columns[...])
    state = planes_of(lower, upper)
    for layer in range(2):
        stiffness = stiffness_of(viscosity, facts, layer)
        new = moved(layer, state, below_halo, above_halo, forcing, stiffness, rims)
        for k in range(3):
            new_velocity[k, layer] = new[k]
        share = stiffness * sum(new[k] * stress[k, layer] for k in range(3))
        partial[...] = share if layer == 0 else (partial[...] + share) * (1.0 / 96.0)


def last_heat_kernel(
    lower, upper, below_halo, above_halo, edge_rows, columns, flow, velocity_near,
    new_velocity, new_heat, heat, sems,
):
    copies = []

    def send(source, target):
        copies.append(pltpu.make_async_copy(source, target, sems.at[len(copies)]))
        copies[-1].start()

    send(velocity_near, new_velocity)
    rims = (edge_rows[0:8, :], edge_rows[8:16, :], columns[...])
    state = planes_of(lower, upper)
    for layer in range(2):
        heat[layer] = warmed(layer, state, below_halo, above_halo, flow, rims)
        send(heat.at[layer], new_heat.at[layer])
    for copy in copies:
        copy.wait()


VMEM = pl.BlockSpec(memory_space=pltpu.VMEM)
FAR = pl.BlockSpec(memory_space=pltpu.HBM)


def call(kernel, outs, near, far=(), scratch=(), out_specs=None, flops=0):
    far = [pltpu.with_memory_space_constraint(a, pltpu.HBM) for a in far]
    arrays = (*near, *far)
    moved_bytes = 4 * sum(a.size for a in arrays)
    return pl.pallas_call(
        kernel,
        out_shape=[jax.ShapeDtypeStruct(shape, jnp.float32) for shape in outs],
        in_specs=[VMEM] * len(near) + [FAR] * len(far),
        out_specs=out_specs or [VMEM] * len(outs),
        scratch_shapes=list(scratch),
        compiler_params=pltpu.CompilerParams(vmem_limit_bytes=VMEM_BYTES),
        cost_estimate=pl.CostEstimate(
            flops=flops, bytes_accessed=moved_bytes, transcendentals=0
        ),
    )(*arrays)


def over_tiles(array, to):
    count = lax.axis_size("cap")
    return lax.ppermute(array, "cap", [(i, to(i) % count) for i in range(count)])


def of_chip(array):
    count = lax.axis_size("cap")
    pairs = [[i, i + 1] for i in range(0, count, 2)]
    return lax.all_gather(array, "cap", axis_index_groups=pairs)


def to_outer(array):
    return over_tiles(array, lambda i: i + 1 if i % 2 else i - 1)


def along(array, by):
    count = lax.axis_size("rad")
    return lax.ppermute(
        array, "rad", [(i, i + by) for i in range(count) if 0 <= i + by < count]
    )


def radial(lower, upper):
    return along(upper, 1), along(lower, -1)


def shards(
    adjoint_velocity, adjoint_heat, forcing, flow_velocity, forward_stress, viscosity, layer_mask,
    face_flips,
):
    size = adjoint_velocity.shape[-1]
    quarter = lax.axis_size("cap") // 4
    velocity, heat = adjoint_velocity[:, :, 0], adjoint_heat[:, 0]
    forces, flow, stress, visc = (
        forcing[:, :, 0], flow_velocity[:, :, 0], forward_stress[:, :, 0], viscosity[:, 0]
    )
    flips = face_flips.T
    f32 = jnp.float32
    lower, upper, row_own, gift, col_own, facts = call(
        pack_kernel,
        [(4 * size, size)] * 2
        + [(ROW_MESSAGE, size), (ROW_MESSAGE + 8, size), (8, size), (16, size)],
        (),
        (velocity, heat, layer_mask, flips, forces, flow, visc),
        (
            pltpu.SMEM(layer_mask.shape, jnp.int32),
            pltpu.VMEM(flips.shape, jnp.int32),
            pltpu.VMEM((2, 3, 2, 8, size), f32),
            pltpu.VMEM((2, 3, 2, 8, size), f32),
            pltpu.VMEM((2, 2, 8, size), f32),
            pltpu.VMEM((2, ROW_MESSAGE, size), f32),
            pltpu.VMEM((16, size), f32),
            pltpu.SemaphoreType.DMA((10,)),
            pltpu.SemaphoreType.DMA((6,)),
        ),
    )
    halos = radial(lower, upper)
    gifts = of_chip(gift)
    core = lax.rem(lax.axis_index("cap"), 2)
    given = lax.dynamic_index_in_dim(gifts, 1 - core, 0, keepdims=False)[:ROW_MESSAGE]
    got = over_tiles(
        jnp.concatenate([row_own, given]),
        lambda i: i - quarter - 1 if i % 2 else i + quarter + 1,
    )
    outer = to_outer(col_own)
    passed = of_chip(got[:ROW_MESSAGE])
    lower, upper, col_given, col_own, kept = call(
        first_kernel,
        [(4 * size + 16, size)] * 2 + [(16, size)] * 2 + [(2 * KEPT + 16, size)],
        (facts, lower, upper, *halos, gifts, got, passed, outer, forces, visc, flow),
        (),
        (pltpu.VMEM((16, size), f32),),
    )
    halos = radial(lower, upper)
    gifts = of_chip(col_given)
    outer = to_outer(col_own)
    velocity_near, partial, edge_rows, columns = call(
        last_velocity_kernel,
        [velocity.shape, (size, size), (16, size), (size, size)],
        (facts, lower, upper, *halos, gifts, outer, kept, forces, visc, stress),
        (),
        (pltpu.VMEM((16, size), f32),),
    )
    pieces = lax.all_to_all(partial, "rad", 0, 0, tiled=True)
    new_velocity, new_heat = call(
        last_heat_kernel,
        [velocity.shape, heat.shape],
        (lower, upper, *halos, edge_rows, columns, flow, velocity_near),
        (),
        (pltpu.VMEM(heat.shape, f32), pltpu.SemaphoreType.DMA((3,))),
        [FAR, FAR],
    )
    pieces, new_heat = lax.optimization_barrier((pieces, new_heat))
    count = lax.axis_size("rad")
    gradient = jnp.sum(pieces.reshape(count, size // count, size), axis=0)
    return new_velocity[:, :, None], new_heat[:, None], gradient[None]


def solution(mesh):
    fields = P(None, "rad", "cap", None, None)
    scalar_field = P("rad", "cap", None, None)
    return jax.shard_map(
        shards,
        mesh=mesh,
        in_specs=(
            fields, scalar_field, fields, fields, fields, scalar_field, P("rad"), P(),
        ),
        out_specs=(fields, scalar_field, P("cap", "rad", None)),
        check_vma=False,
    )
```
